32 devices in a mesh: grp: 2 (over x), probe: 8 (over z, y), beam: 2 (over core).
Axes of the slice: x: 2, y: 2, z: 4, core: 2. Of those that a mesh axis runs over, the one named last changes fastest.
Arguments:
- smatrix: bfloat16 [8192, 8, 512], P(('grp', 'beam'), 'probe'), parts along dimension 0, may hold values from -0.09375 to 0.09375
- aperture: float32 [4096], P('beam'), may hold values from 0.5 to 1.5
- aberration: float32 [4096], P('beam'), may hold values from -3.140625 to 3.140625
- beam_k: int32 [2, 4096], P(None, 'beam'), may hold values from -32 to 31, as said below
- probe_pos: int32 [2, 2048], P(None, 'probe'), may hold values from 0 to 1023
- patches: bfloat16 [128, 512], P(('grp', 'probe')), parts along dimension 0, may hold values from -6 to 6
- patch_col: int32 [128], P('grp'), parts along dimension 0, may hold values from 0 to 7, never falling along the last dimension, each value on 1 to 32 neighbouring positions
Outputs:
- ionization: float32 [16, 2048], P('grp', ('probe', 'beam')), parts along dimension 0
The draws below stay inside these ranges and needn't reach their ends.
There are 2 independent parts, one for each index of `grp`. The reference program is written for one: setup_inputs(seed, part) draws one part's arguments, and reference() takes and returns one part's arrays. A program takes and returns all parts, laid end to end along the dimension named above; an argument that names none is the same for every part. Nothing has to cross between parts.
Inputs may be any that keep to these rules, and one draw needn't show every extreme that they name: `patch_col`: patches are ordered by atom column; each of the 8 columns has 1 to 32 patches, and some column has exactly 32. `beam_k`: no two beams have the same pair of indices.
All inputs are finite; a program needn't handle non-finite values.
Results may differ from the reference program's by a relative error of at most 0.005.
Values may be sent and summed in bfloat16 or wider, within the bound.
No kernel may reach another device: no remote copies, remote signals or barrier semaphores. Data moves between devices by JAX's collectives and lax.ppermute only.
A program may use at most 128 MiB of HBM per device.

```python
import math
import jax
import jax.numpy as jnp
import numpy as np
from jax import lax

NB = 4096
PSIDE = 16
PIX = 256
GRID = 1024
KMAX = 32
NCOL = 8
NPATCH = 64
MOSTP = 32
PTOT = 2048


def draw_beam_k(key, part):
    side_count = 2 * KMAX
    total_points = side_count * side_count
    rank_score = jax.random.permutation(jax.random.fold_in(key, 11), total_points).astype(jnp.int32) + 2
    grid_index = jnp.arange(total_points, dtype=jnp.int32)
    rank_score = jnp.where(grid_index == 0, 0, rank_score)
    rank_score = jnp.where(grid_index == total_points - 1, 1, rank_score)
    chosen_points = jnp.argsort(rank_score, stable=True)[:NB].astype(jnp.int32)
    shuffled = jax.random.permutation(jax.random.fold_in(key, 23), chosen_points).astype(jnp.int32)
    first_index = shuffled // side_count - KMAX
    second_index = shuffled % side_count - KMAX
    return jnp.stack([first_index, second_index]).astype(jnp.int32)


def touch_ends(values, own_key, low, largest):
    place = [jax.random.randint(jax.random.fold_in(own_key, axis), (), 0, length) for axis, length in enumerate(values.shape)]
    main_axis = values.shape.index(max(values.shape))
    neighbour = place[:main_axis] + [(place[main_axis] + 1) % values.shape[main_axis]] + place[main_axis + 1:]
    return values.at[tuple(place)].set(low).at[tuple(neighbour)].set(largest)


def levels(rng, extent, cuts, low, high):
    level, own = 1.0, jax.random.fold_in(rng, 6)
    for position, shards_of in cuts:
        heights = jnp.exp(jax.random.uniform(jax.random.fold_in(own, position), (shards_of,), jnp.float32, low / len(cuts), high / len(cuts)))
        level = level * jnp.repeat(heights, extent[position] // shards_of).reshape([-1 if axis == position else 1 for axis in range(len(extent))])
    return level


def split_up(number_of, total, most, skew):
    weights = [(1 << 20) // math.isqrt(rank ** skew) + 1 for rank in range(2, number_of + 1)]
    spare, counts = total - most - (number_of - 1), [1] * (number_of - 1)
    while spare > 0:
        free = [i for i in range(number_of - 1) if counts[i] < most]
        whole, remaining = sum([weights[i] for i in free]), spare
        for i in free:
            extra = min(most - counts[i], max(1, remaining * weights[i] // whole), spare)
            counts[i] = counts[i] + extra
            spare = spare - extra
    return np.array([most] + counts)


def ragged_sizes(own_key, count, total, limit, skew):
    if count == 2:
        one = jax.random.randint(own_key, (), max(1, total - limit), min(limit, total - 1) + 1)
        return jnp.stack([one, total - one])
    lengths = jnp.asarray(split_up(count, total, limit, skew), jnp.int32)
    pairs = (count - 1) // 2
    giver, receiver = lengths[1:1 + 2 * pairs:2], lengths[2:2 + 2 * pairs:2]
    margin = jnp.minimum(giver - 1, limit - receiver)
    moved = jax.random.randint(jax.random.fold_in(own_key, 1), (pairs,), 0, 1 << 20) % (margin + 1)
    lengths = lengths.at[1:1 + 2 * pairs:2].set(giver - moved).at[2:2 + 2 * pairs:2].set(receiver + moved)
    return lengths[jax.random.permutation(jax.random.fold_in(own_key, 2), count)]


def bell_draw(stream_key, shape, deviation, most, pieces=(), kind=jnp.bfloat16):
    factor_of = levels(stream_key, shape, pieces, -0.22, 0.18) if pieces else 1.0
    values = jax.random.normal(stream_key, shape, jnp.float32) * deviation * factor_of
    return jnp.minimum(jnp.maximum(values, -most), most).astype(kind)


def setup_inputs(seed: int = 0, part: int = 0) -> dict:
    arg_keys = jax.random.split(jax.random.key(seed), 8)
    part_keys = jax.random.split(jax.random.fold_in(arg_keys[7], part), 8)
    smatrix = bell_draw(part_keys[0], (NB, NCOL, 2 * PIX), NB ** -0.5, 0.09375, ((0, 2), (1, 8)))
    aperture = jnp.clip(0.5 + 1.0 * jax.random.uniform(arg_keys[1], (NB,), jnp.float32) ** levels(arg_keys[1], (NB,), ((0, 2),), -0.2, 0.2), 0.5, 1.5)
    aberration = jnp.clip(jax.random.uniform(arg_keys[2], (NB,), jnp.float32, -3.140625, 3.140625), -3.140625, 3.140625)
    beam_k = draw_beam_k(jax.random.fold_in(arg_keys[7], 71), part)
    probe_pos = touch_ends(jax.random.randint(arg_keys[4], (2, PTOT), 0, GRID), jax.random.fold_in(arg_keys[4], 1), 0, GRID - 1).astype(jnp.int32)
    patches = bell_draw(part_keys[5], (NPATCH, 2 * PIX), 1.0, 6.0, ((0, 8),))
    patch_col = jnp.searchsorted(jnp.cumsum(ragged_sizes(part_keys[6], NCOL, NPATCH, MOSTP, 2)), jnp.arange(NPATCH), side="right").astype(jnp.int32)
    return dict(smatrix=smatrix, aperture=aperture, aberration=aberration, beam_k=beam_k, probe_pos=probe_pos, patches=patches, patch_col=patch_col)


def coefficients(beam_k, aperture, aberration, positions):
    turn_count = jnp.mod(positions[0][:, None] * beam_k[0][None, :] + positions[1][:, None] * beam_k[1][None, :], GRID)
    phase_angle = aberration[None, :] + (2.0 * math.pi / GRID) * turn_count.astype(jnp.float32)
    real_coef = (aperture[None, :] * jnp.cos(phase_angle)).astype(jnp.bfloat16)
    imag_coef = (-(aperture[None, :] * jnp.sin(phase_angle))).astype(jnp.bfloat16)
    return real_coef, imag_coef


def detector(edge_count):
    half_side = edge_count // 2
    pixel_index = jnp.arange(edge_count * edge_count, dtype=jnp.int32)
    mode_index = jnp.arange(edge_count * half_side, dtype=jnp.int32)
    row_off = pixel_index // edge_count
    col_off = pixel_index % edge_count
    freq_first = mode_index // half_side - half_side
    freq_second = mode_index % half_side - edge_count // 4
    turn_count = jnp.mod(row_off[:, None] * freq_first[None, :] + col_off[:, None] * freq_second[None, :], edge_count)
    angle_value = (2.0 * math.pi / edge_count) * turn_count.astype(jnp.float32)
    real_part = jnp.cos(angle_value)
    imag_part = -jnp.sin(angle_value)
    upper_rows = jnp.concatenate([real_part, imag_part], axis=1)
    lower_rows = jnp.concatenate([-imag_part, real_part], axis=1)
    return jnp.concatenate([upper_rows, lower_rows], axis=0).astype(jnp.bfloat16)


def patch_energy(picked, pot_rows, det_table):
    half_width = pot_rows.shape[-1] // 2
    psi_re = picked[..., :half_width].astype(jnp.float32)
    psi_im = picked[..., half_width:].astype(jnp.float32)
    pot_re = pot_rows[:, :half_width].astype(jnp.float32)
    pot_im = pot_rows[:, half_width:].astype(jnp.float32)
    wave_out = jnp.concatenate([psi_re * pot_re - psi_im * pot_im, psi_re * pot_im + psi_im * pot_re], axis=-1).astype(jnp.bfloat16)
    projected = jnp.einsum("rjx,xq->rjq", wave_out.astype(jnp.float32), det_table.astype(jnp.float32))
    return jnp.sum(projected * projected, axis=-1) / float(half_width * (det_table.shape[1] // 2))


def reference(smatrix, aperture, aberration, beam_k, probe_pos, patches, patch_col):
    det_table = detector(PSIDE)
    half_width = smatrix.shape[2] // 2
    flat_matrix = smatrix.reshape(NB, NCOL * 2 * half_width)
    block_rows = math.gcd(PTOT, 512)
    pos_blocks = probe_pos.reshape(2, PTOT // block_rows, block_rows).transpose(1, 0, 2)
    onehot = (patch_col[:, None] == jnp.arange(NCOL, dtype=jnp.int32)[None, :]).astype(jnp.float32)

    def per_block(positions):
        real_coef, imag_coef = coefficients(beam_k, aperture, aberration, positions)
        from_re = jnp.dot(real_coef, flat_matrix, preferred_element_type=jnp.float32).reshape(block_rows, NCOL, 2 * half_width)
        from_im = jnp.dot(imag_coef, flat_matrix, preferred_element_type=jnp.float32).reshape(block_rows, NCOL, 2 * half_width)
        psi = jnp.concatenate([from_re[..., :half_width] - from_im[..., half_width:], from_re[..., half_width:] + from_im[..., :half_width]], axis=-1).astype(jnp.bfloat16)
        picked = jnp.take(psi, patch_col, axis=1)
        energy = patch_energy(picked, patches, det_table)
        return jnp.dot(energy, onehot, precision=lax.Precision.HIGHEST)

    result = lax.map(per_block, pos_blocks)
    return result.reshape(PTOT, NCOL).T
```

```python
import functools
import math

import jax
import jax.numpy as jnp
import numpy as np
from jax import lax
from jax.experimental import pallas as pl
from jax.experimental.pallas import tpu as pltpu
from jax.sharding import PartitionSpec as P

PSIDE = 16
GRID = 1024
KMAX = 32
LANE = 128


def mode_overlap():
    pix = np.arange(LANE)
    row, col = pix // PSIDE, pix % PSIDE
    dist = col[:, None] - col[None, :]
    freq = np.arange(PSIDE // 2) - PSIDE // 4
    angle = (2.0 * math.pi / PSIDE) * ((freq[:, None, None] * dist[None]) % PSIDE)
    same = (row[:, None] == row[None, :]).astype(np.float64) * PSIDE / float(PSIDE**2 * (PSIDE**2 // 2))
    return np.stack([np.cos(angle).sum(0) * same, -np.sin(angle).sum(0) * same]).astype(np.float32)


def half_turns(count):
    folded = jnp.bitwise_and(count + GRID, 2 * GRID - 1) - GRID
    u = folded.astype(jnp.float32) * (1.0 / GRID)
    u2 = u * u
    terms = 9
    c = [(-1.0) ** k * math.pi ** (2 * k) / math.factorial(2 * k) for k in range(terms)]
    s = [(-1.0) ** k * math.pi ** (2 * k + 1) / math.factorial(2 * k + 1) for k in range(terms)]
    cos_v, sin_v = jnp.full_like(u, c[-1]), jnp.full_like(u, s[-1])
    for k in range(terms - 2, -1, -1):
        cos_v = cos_v * u2 + c[k]
        sin_v = sin_v * u2 + s[k]
    return cos_v, sin_v * u


def kernel(
    rows, blocks, s_own, s_rem, amp, abr, k_own, k_rem, shared, cols, overlap, out,
    s_all, x_even, x_odd, grid_rows, coef, basis, tab, phase, place_v, place_s, sem_s, sem_i,
):
    f32, bf16 = jnp.float32, jnp.bfloat16
    half = lax.axis_index("beam")
    column = lax.axis_index("probe")
    copies = [
        pltpu.make_async_copy(src, s_all.at[pl.ds(i * rows, rows)], sem_s.at[i])
        for i, src in enumerate((s_own, s_rem))
    ]
    for c in copies:
        c.start()
    for i, k_ref in enumerate((k_own, k_rem)):
        kx, ky = k_ref[0:1, :], k_ref[1:2, :]
        qx, qy = kx >= 0, ky >= 0
        mx, my = jnp.where(qx, kx, -1 - kx), jnp.where(qy, ky, -1 - ky)
        quad = 2 * qx.astype(jnp.int32) + qy.astype(jnp.int32)
        place_v[i : i + 1, :] = ((quad * KMAX + mx) * KMAX + my) * 4
    idx_copy = pltpu.make_async_copy(place_v, place_s, sem_i)
    idx_copy.start()
    phase[0] = amp[...] * jnp.cos(abr[...])
    phase[1] = amp[...] * jnp.sin(abr[...])

    def tables(j):
        px = shared[j, 8:9, pl.ds(pl.multiple_of(half * LANE, LANE), LANE)].astype(jnp.int32)
        py = shared[j, 8:9, pl.ds(pl.multiple_of(2 * LANE + half * LANE, LANE), LANE)].astype(jnp.int32)
        my = lax.broadcasted_iota(jnp.int32, (KMAX, LANE), 0)
        mx = lax.broadcasted_iota(jnp.int32, (8, LANE), 0)
        cy, sy = half_turns((2 * my + 1) * py)
        cx, sx = half_turns(jnp.where(mx < 4, 2 * mx + 1, 8) * px)
        reps = LANE // KMAX
        spread = lambda t: jnp.concatenate([jnp.broadcast_to(t[m : m + 1], (KMAX, LANE)) for m in range(reps)], 0)
        made = (
            jnp.concatenate([cy] * reps, 0), jnp.concatenate([sy] * reps, 0), spread(cx), spread(sx),
            jnp.broadcast_to(cx[4:5], (LANE, LANE)), jnp.broadcast_to(sx[4:5], (LANE, LANE)),
        )
        for n, t in enumerate(made):
            tab[n, pl.ds(pl.multiple_of(j * LANE, LANE), LANE), :] = t.T

    def coefficients(j, sub, step=32):
        here = pl.ds(pl.multiple_of(j * LANE + sub * step, step), step)
        cy, sy, cx, sx, c4, s4 = (tab[n, here, :] for n in range(6))
        for g in range(KMAX // 4):
            prods = (cx * cy, sx * sy, sx * cy, cx * sy)
            for n, v in enumerate(prods):
                coef[here, pl.ds((4 * g + n) * LANE, LANE)] = v.astype(bf16)
            cx, sx = cx * c4 - sx * s4, sx * c4 + cx * s4

    def turned(r, x_ref):
        here = pl.ds(pl.multiple_of(r * LANE, LANE), LANE)
        ph_c = jnp.broadcast_to(phase[0, pl.ds(r, 1), :], (LANE, LANE)).T
        ph_s = jnp.broadcast_to(phase[1, pl.ds(r, 1), :], (LANE, LANE)).T
        for h in range(2):
            re = s_all[here, pl.ds(h * LANE, LANE)].astype(f32)
            im = s_all[here, pl.ds((2 + h) * LANE, LANE)].astype(f32)
            x_ref[pl.ds(h, LANE, stride=4), :] = ph_c * re + ph_s * im
            x_ref[pl.ds(2 + h, LANE, stride=4), :] = ph_c * im - ph_s * re

    def scatter(r, x_ref):
        per = rows // LANE
        which, base = r // per, (r % per) * LANE
        for u in range(LANE):
            to = place_s[which, base + u]
            grid_rows[pl.ds(pl.multiple_of(to, 4), 4), :] = x_ref[4 * u : 4 * u + 4, :]

    total = 2 * rows // LANE
    tables(0)
    for c in copies:
        c.wait()
    idx_copy.wait()
    turned(0, x_even)
    per_step = total // blocks

    @pl.loop(0, blocks)
    def _(j):
        for u in range(per_step):
            r = j * per_step + u
            now, later = (x_even, x_odd) if u % 2 == 0 else (x_odd, x_even)
            turned(jnp.minimum(r + 1, total - 1), later)
            scatter(r, now)
        for sub in range(4):
            coefficients(j, sub)
        tables(jnp.minimum(j + 1, blocks - 1))

    quarter = KMAX * KMAX * 4

    @pl.loop(0, KMAX * KMAX // LANE)
    def _(g):
        to = lambda n: pl.ds(pl.multiple_of((4 * g + n) * LANE, LANE), LANE)
        for h in range(2):
            vals = []
            for part in range(2):
                mm, mp, pm, pp = (
                    grid_rows[pl.ds(q * quarter + g * 4 * LANE + 2 * part + h, LANE, stride=4), :] for q in range(4)
                )
                a, b, c, d = pp + mm, pp - mm, pm + mp, pm - mp
                vals.append((a + c, c - a, b + d, b - d))
            re, im = vals
            at_re, at_im = pl.ds(2 * h * LANE, LANE), pl.ds((2 * h + 1) * LANE, LANE)
            for n in range(4):
                if n < 2:
                    basis[to(n), at_re], basis[to(n), at_im] = re[n].astype(bf16), im[n].astype(bf16)
                else:
                    basis[to(n), at_re], basis[to(n), at_im] = im[n].astype(bf16), (-re[n]).astype(bf16)

    pots = jnp.concatenate([shared[j, 0:8, :] for j in range(blocks)], 0)
    mine = (cols[...] == column).astype(f32)
    left = (pots.T * mine).astype(bf16)
    right = pots.astype(bf16)
    g_re, g_im = overlap[0], overlap[1]
    energy = []
    for h in range(2):
        lr, li = left[h * LANE : (h + 1) * LANE], left[(2 + h) * LANE : (3 + h) * LANE]
        rr, ri = right[:, h * LANE : (h + 1) * LANE], right[:, (2 + h) * LANE : (3 + h) * LANE]
        mul = lambda a, b: jnp.dot(a, b, preferred_element_type=f32)
        r_re, r_im = mul(lr, rr) + mul(li, ri), mul(li, rr) - mul(lr, ri)
        h_re, h_im = g_re * r_re - g_im * r_im, g_re * r_im + g_im * r_re
        form = jnp.concatenate(
            [jnp.concatenate([h_re, h_im], 1), jnp.concatenate([-h_im, h_re], 1)], 0
        ).astype(bf16)
        psi = jnp.dot(coef[...], basis[:, pl.ds(2 * h * LANE, 2 * LANE)], preferred_element_type=f32)
        e = psi * jnp.dot(psi.astype(bf16), form, preferred_element_type=f32)
        energy.append(e[:, :LANE] + e[:, LANE:])
    e = energy[0] + energy[1]
    for j in range(blocks):
        out[j : j + 1, :] = jnp.sum(e[j * LANE : (j + 1) * LANE].T, axis=0, keepdims=True)


def shards(smatrix, aperture, aberration, beam_k, probe_pos, patches, patch_col):
    blocks = lax.axis_size("probe")
    rows, width = smatrix.shape[0], smatrix.shape[2]
    swap = lambda v: lax.ppermute(v, "beam", [(0, 1), (1, 0)])
    s_own = smatrix.reshape(rows, width)
    s_rem = swap(s_own)
    k_rem = swap(beam_k)
    weights = jnp.stack([aperture, aberration])
    both = jnp.concatenate([weights, swap(weights)], 1).reshape(2, 2 * rows // LANE, LANE)
    small = jnp.concatenate([patches.astype(jnp.float32), probe_pos.astype(jnp.float32).reshape(1, width)], 0)
    shared = lax.all_to_all(jnp.broadcast_to(small[None], (blocks,) + small.shape), "probe", 0, 0)
    vmem, anyw = pl.BlockSpec(memory_space=pltpu.VMEM), pl.BlockSpec(memory_space=pl.ANY)
    probes = blocks * LANE
    grid = 4 * KMAX * KMAX
    energy = pl.pallas_call(
        functools.partial(kernel, rows, blocks),
        out_shape=jax.ShapeDtypeStruct((blocks, LANE), jnp.float32),
        in_specs=[anyw, anyw] + [vmem] * 7,
        out_specs=vmem,
        scratch_shapes=[
            pltpu.VMEM((2 * rows, width), jnp.bfloat16),
            pltpu.VMEM((4 * LANE, LANE), jnp.float32),
            pltpu.VMEM((4 * LANE, LANE), jnp.float32),
            pltpu.VMEM((4 * grid, LANE), jnp.float32),
            pltpu.VMEM((probes, grid), jnp.bfloat16),
            pltpu.VMEM((grid, width), jnp.bfloat16),
            pltpu.VMEM((6, probes, LANE), jnp.float32),
            pltpu.VMEM((2, 2 * rows // LANE, LANE), jnp.float32),
            pltpu.VMEM((2, rows), jnp.int32),
            pltpu.SMEM((2, rows), jnp.int32),
            pltpu.SemaphoreType.DMA((2,)),
            pltpu.SemaphoreType.DMA,
        ],
        compiler_params=pltpu.CompilerParams(vmem_limit_bytes=56 * 1024 * 1024),
    )(
        s_own, s_rem, both[0], both[1], beam_k, k_rem, shared, patch_col.reshape(1, -1),
        jnp.asarray(mode_overlap()),
    )
    return lax.all_to_all(energy, "probe", 0, 0, tiled=True)


def solution(mesh):
    placed = (
        P(("grp", "beam"), "probe", None),
        P("beam"),
        P("beam"),
        P(None, "beam"),
        P(None, "probe"),
        P(("grp", "probe"), None),
        P("grp"),
    )
    return jax.shard_map(
        shards, mesh=mesh, in_specs=placed, out_specs=P("grp", ("probe", "beam")), check_vma=False
    )
```

```python
import functools
import math

import jax
import jax.numpy as jnp
import numpy as np
from jax import lax
from jax.experimental import pallas as pl
from jax.experimental.pallas import tpu as pltpu
from jax.sharding import PartitionSpec as P

PSIDE = 16
GRID = 1024
KMAX = 32
LANE = 128


def mode_overlap():
    pix = np.arange(LANE)
    row, col = pix // PSIDE, pix % PSIDE
    dist = col[:, None] - col[None, :]
    freq = np.arange(PSIDE // 2) - PSIDE // 4
    angle = (2.0 * math.pi / PSIDE) * ((freq[:, None, None] * dist[None]) % PSIDE)
    same = (row[:, None] == row[None, :]).astype(np.float64) * PSIDE / float(PSIDE**2 * (PSIDE**2 // 2))
    return np.stack([np.cos(angle).sum(0) * same, -np.sin(angle).sum(0) * same]).astype(np.float32)


def half_turns(count):
    folded = jnp.bitwise_and(count + GRID, 2 * GRID - 1) - GRID
    u = folded.astype(jnp.float32) * (1.0 / GRID)
    u2 = u * u
    terms = 9
    c = [(-1.0) ** k * math.pi ** (2 * k) / math.factorial(2 * k) for k in range(terms)]
    s = [(-1.0) ** k * math.pi ** (2 * k + 1) / math.factorial(2 * k + 1) for k in range(terms)]
    cos_v, sin_v = jnp.full_like(u, c[-1]), jnp.full_like(u, s[-1])
    for k in range(terms - 2, -1, -1):
        cos_v = cos_v * u2 + c[k]
        sin_v = sin_v * u2 + s[k]
    return cos_v, sin_v * u


def place_rows(k_ref, place_v):
    kx, ky = k_ref[0:1, :], k_ref[1:2, :]
    qx, qy = kx >= 0, ky >= 0
    mx, my = jnp.where(qx, kx, -1 - kx), jnp.where(qy, ky, -1 - ky)
    quad = 2 * qx.astype(jnp.int32) + qy.astype(jnp.int32)
    place_v[...] = ((quad * KMAX + mx) * KMAX + my) * 4


def spread_rows(s_ref, amp, abr, k_ref, grid_rows, x_even, x_odd, phase, place_v, place_s, sem, ready=None):
    f32 = jnp.float32
    rows = s_ref.shape[0]
    place_rows(k_ref, place_v)
    idx_copy = pltpu.make_async_copy(place_v.at[0], place_s, sem)
    idx_copy.start()
    phase[0] = amp[...] * jnp.cos(abr[...])
    phase[1] = amp[...] * jnp.sin(abr[...])

    def turned(r, x_ref):
        here = pl.ds(pl.multiple_of(r * LANE, LANE), LANE)
        ph_c = jnp.broadcast_to(phase[0, pl.ds(r, 1), :], (LANE, LANE)).T
        ph_s = jnp.broadcast_to(phase[1, pl.ds(r, 1), :], (LANE, LANE)).T
        for h in range(2):
            re = s_ref[here, pl.ds(h * LANE, LANE)].astype(f32)
            im = s_ref[here, pl.ds((2 + h) * LANE, LANE)].astype(f32)
            x_ref[pl.ds(h, LANE, stride=4), :] = ph_c * re + ph_s * im
            x_ref[pl.ds(2 + h, LANE, stride=4), :] = ph_c * im - ph_s * re

    def scatter(r, x_ref):
        base = r * LANE
        for u in range(LANE):
            to = pl.multiple_of(place_s[base + u], 4)
            grid_rows[pl.ds(to, 4), :] = x_ref[4 * u : 4 * u + 4, :]

    if ready is not None:
        ready()
    turned(0, x_even)
    idx_copy.wait()
    total = rows // LANE

    @pl.loop(0, total // 2)
    def _(i):
        r = 2 * i
        turned(r + 1, x_odd)
        scatter(r, x_even)
        turned(jnp.minimum(r + 2, total - 1), x_even)
        scatter(r + 1, x_odd)


def own_kernel(s_own, amp, abr, k_ref, grid_rows, s_vmem, x_even, x_odd, phase, place_v, place_s, sem, sem_s):
    load = pltpu.make_async_copy(s_own, s_vmem, sem_s)
    load.start()
    spread_rows(s_vmem, amp, abr, k_ref, grid_rows, x_even, x_odd, phase, place_v, place_s, sem, load.wait)


def other_kernel(
    held, s_rem, amp, abr, k_ref, grid_rows, basis, x_even, x_odd, phase, place_v, place_s, sem
):
    bf16 = jnp.bfloat16
    spread_rows(s_rem, amp, abr, k_ref, grid_rows, x_even, x_odd, phase, place_v, place_s, sem)
    quarter = KMAX * KMAX * 4

    @pl.loop(0, KMAX * KMAX // LANE)
    def _(g):
        to = lambda n: pl.ds(pl.multiple_of((4 * g + n) * LANE, LANE), LANE)
        for h in range(2):
            vals = []
            for part in range(2):
                mm, mp, pm, pp = (
                    grid_rows[pl.ds(q * quarter + g * 4 * LANE + 2 * part + h, LANE, stride=4), :] for q in range(4)
                )
                a, b, c, d = pp + mm, pp - mm, pm + mp, pm - mp
                vals.append((a + c, c - a, b + d, b - d))
            re, im = vals
            at_re, at_im = pl.ds(2 * h * LANE, LANE), pl.ds((2 * h + 1) * LANE, LANE)
            for n in range(4):
                if n < 2:
                    basis[to(n), at_re], basis[to(n), at_im] = re[n].astype(bf16), im[n].astype(bf16)
                else:
                    basis[to(n), at_re], basis[to(n), at_im] = im[n].astype(bf16), (-re[n]).astype(bf16)


def probe_kernel(blocks, basis, near, far, cols, overlap, out, coef_even, coef_odd, tab, pots):
    f32, bf16 = jnp.float32, jnp.bfloat16
    half, column = lax.axis_index("beam"), lax.axis_index("probe")
    step = coef_even.shape[0]
    per = step // LANE

    def tables(j, source, i):
        hi = source[i, 8:9, :].astype(f32).astype(jnp.int32)
        lo = source[i, 9:10, :].astype(f32).astype(jnp.int32)
        pos = 32 * hi + lo
        width = pos.shape[1] // 4
        px = jnp.where(half == 0, pos[:, :width], pos[:, width : 2 * width])
        py = jnp.where(half == 0, pos[:, 2 * width : 3 * width], pos[:, 3 * width :])
        my = lax.broadcasted_iota(jnp.int32, (KMAX, LANE), 0)
        mx = lax.broadcasted_iota(jnp.int32, (8, LANE), 0)
        cy, sy = half_turns((2 * my + 1) * py)
        cx, sx = half_turns(jnp.where(mx < 4, 2 * mx + 1, 8) * px)
        reps = LANE // KMAX
        spread = lambda t: jnp.concatenate([jnp.broadcast_to(t[m : m + 1], (KMAX, LANE)) for m in range(reps)], 0)
        made = (
            jnp.concatenate([cy] * reps, 0), jnp.concatenate([sy] * reps, 0), spread(cx), spread(sx),
            jnp.broadcast_to(cx[4:5], (LANE, LANE)), jnp.broadcast_to(sx[4:5], (LANE, LANE)),
        )
        for n, t in enumerate(made):
            tab[n, j * LANE : (j + 1) * LANE, :] = t.T

    def coefficients(m, coef, sub=32):
        for row in range(0, step, sub):
            cy, sy, cx, sx, c4, s4 = (tab[n, m * step + row : m * step + row + sub, :] for n in range(6))
            for g in range(KMAX // 4):
                prods = (cx * cy, sx * sy, sx * cy, cx * sy)
                for n, v in enumerate(prods):
                    coef[row : row + sub, (4 * g + n) * LANE : (4 * g + n + 1) * LANE] = v.astype(bf16)
                cx, sx = cx * c4 - sx * s4, sx * c4 + cx * s4

    def prepare(m, coef):
        for j in range(m * per, (m + 1) * per):
            tables(j, near if j < blocks // 2 else far, j % (blocks // 2))
        coefficients(m, coef)

    for j in range(blocks):
        source = near if j < blocks // 2 else far
        owner = column ^ j
        pots[pl.ds(pl.multiple_of(owner * 8, 8), 8), :] = source[j % (blocks // 2), 0:8, :].astype(f32)
    mine = (cols[...] == column).astype(f32)
    left = (pots[...].T * mine).astype(bf16)
    right = pots[...].astype(bf16)
    g_re, g_im = overlap[0], overlap[1]
    mul = lambda a, b: jnp.dot(a, b, preferred_element_type=f32)
    forms = []
    for h in range(2):
        lr, li = left[h * LANE : (h + 1) * LANE], left[(2 + h) * LANE : (3 + h) * LANE]
        rr, ri = right[:, h * LANE : (h + 1) * LANE], right[:, (2 + h) * LANE : (3 + h) * LANE]
        r_re, r_im = mul(lr, rr) + mul(li, ri), mul(li, rr) - mul(lr, ri)
        h_re, h_im = g_re * r_re - g_im * r_im, g_re * r_im + g_im * r_re
        forms.append(
            jnp.concatenate([jnp.concatenate([h_re, h_im], 1), jnp.concatenate([-h_im, h_re], 1)], 0).astype(bf16)
        )

    prepare(0, coef_even)
    steps = blocks * LANE // step
    for m in range(steps):
        now, later = (coef_even, coef_odd) if m % 2 == 0 else (coef_odd, coef_even)
        psi = mul(now[...], basis[...])
        if m + 1 < steps:
            prepare(m + 1, later)
        e = 0.0
        for h in range(2):
            wave = psi[:, 2 * h * LANE : (2 * h + 2) * LANE]
            v = wave * mul(wave.astype(bf16), forms[h])
            e = e + v[:, :LANE] + v[:, LANE:]
        for i in range(per):
            j = m * per + i
            out[pl.ds(column ^ j, 1), :] = jnp.sum(e[i * LANE : (i + 1) * LANE].T, axis=0, keepdims=True)


def shards(smatrix, aperture, aberration, beam_k, probe_pos, patches, patch_col):
    f32, bf16 = jnp.float32, jnp.bfloat16
    blocks = lax.axis_size("probe")
    rows, width = smatrix.shape[0], smatrix.shape[2]
    swap = lambda v: lax.ppermute(v, "beam", [(0, 1), (1, 0)])
    s_own = smatrix.reshape(rows, width)
    s_rem = swap(s_own)
    amp_rem, abr_rem, k_rem = swap(aperture), swap(aberration), swap(beam_k)
    pos = probe_pos.reshape(1, width)
    small = jnp.concatenate(
        [patches, (pos // 32).astype(bf16), (pos % 32).astype(bf16), jnp.zeros((6, width), bf16)], 0
    )[None]
    reach = 1
    while reach < blocks:
        far = lax.ppermute(small, "probe", [(i, i ^ reach) for i in range(blocks)])
        near, reach = small, 2 * reach
        if reach < blocks:
            small = jnp.concatenate([near, far], 0)

    vmem, anyw = pl.BlockSpec(memory_space=pltpu.VMEM), pl.BlockSpec(memory_space=pl.ANY)
    params = pltpu.CompilerParams(vmem_limit_bytes=24 * 1024 * 1024)
    probes, grid = blocks * LANE, 4 * KMAX * KMAX
    turning = [
        pltpu.VMEM((4 * LANE, LANE), f32),
        pltpu.VMEM((4 * LANE, LANE), f32),
        pltpu.VMEM((2, rows // LANE, LANE), f32),
        pltpu.VMEM((1, rows), jnp.int32),
        pltpu.SMEM((rows,), jnp.int32),
        pltpu.SemaphoreType.DMA,
    ]
    tile = lambda v: v.reshape(rows // LANE, LANE)
    cost = lambda n: pl.CostEstimate(flops=n, bytes_accessed=4 * 2**20, transcendentals=0)
    held_shape = jax.ShapeDtypeStruct((4 * grid, LANE), f32)
    held = pl.pallas_call(
        own_kernel,
        out_shape=held_shape,
        in_specs=[anyw] + [vmem] * 3,
        out_specs=vmem,
        scratch_shapes=[pltpu.VMEM((rows, width), bf16)] + turning + [pltpu.SemaphoreType.DMA],
        compiler_params=params,
        cost_estimate=cost(3 * 10**9),
    )(s_own, tile(aperture), tile(aberration), beam_k)
    _, basis = pl.pallas_call(
        other_kernel,
        out_shape=(held_shape, jax.ShapeDtypeStruct((grid, width), bf16)),
        in_specs=[vmem] * 5,
        out_specs=(vmem, vmem),
        scratch_shapes=turning,
        input_output_aliases={0: 0},
        compiler_params=params,
        cost_estimate=cost(4 * 10**9),
    )(held, s_rem, tile(amp_rem), tile(abr_rem), k_rem)
    energy = pl.pallas_call(
        functools.partial(probe_kernel, blocks),
        out_shape=jax.ShapeDtypeStruct((blocks, LANE), f32),
        in_specs=[vmem] * 5,
        out_specs=vmem,
        scratch_shapes=[
            pltpu.VMEM((2 * LANE, grid), bf16),
            pltpu.VMEM((2 * LANE, grid), bf16),
            pltpu.VMEM((6, probes, LANE), f32),
            pltpu.VMEM((patch_col.shape[0], width), f32),
        ],
        compiler_params=params,
        cost_estimate=cost(6 * 10**9),
    )(basis, near, far, patch_col.reshape(1, -1), jnp.asarray(mode_overlap()))
    return lax.all_to_all(energy, "probe", 0, 0, tiled=True)


def solution(mesh):
    placed = (
        P(("grp", "beam"), "probe", None),
        P("beam"),
        P("beam"),
        P(None, "beam"),
        P(None, "probe"),
        P(("grp", "probe"), None),
        P("grp"),
    )
    return jax.shard_map(
        shards, mesh=mesh, in_specs=placed, out_specs=P("grp", ("probe", "beam")), check_vma=False
    )
```

```python
import functools
import math

import jax
import jax.numpy as jnp
import numpy as np
from jax import lax
from jax.experimental import pallas as pl
from jax.experimental.pallas import tpu as pltpu
from jax.sharding import PartitionSpec as P

PSIDE = 16
GRID = 1024
KMAX = 32
LANE = 128


def mode_overlap():
    pix = np.arange(LANE)
    row, col = pix // PSIDE, pix % PSIDE
    dist = col[:, None] - col[None, :]
    freq = np.arange(PSIDE // 2) - PSIDE // 4
    angle = (2.0 * math.pi / PSIDE) * ((freq[:, None, None] * dist[None]) % PSIDE)
    same = (row[:, None] == row[None, :]).astype(np.float64) * PSIDE / float(PSIDE**2 * (PSIDE**2 // 2))
    return np.stack([np.cos(angle).sum(0) * same, -np.sin(angle).sum(0) * same]).astype(np.float32)


def half_turns(count):
    folded = jnp.bitwise_and(count + GRID, 2 * GRID - 1) - GRID
    u = folded.astype(jnp.float32) * (1.0 / GRID)
    u2 = u * u
    terms = 9
    c = [(-1.0) ** k * math.pi ** (2 * k) / math.factorial(2 * k) for k in range(terms)]
    s = [(-1.0) ** k * math.pi ** (2 * k + 1) / math.factorial(2 * k + 1) for k in range(terms)]
    cos_v, sin_v = jnp.full_like(u, c[-1]), jnp.full_like(u, s[-1])
    for k in range(terms - 2, -1, -1):
        cos_v = cos_v * u2 + c[k]
        sin_v = sin_v * u2 + s[k]
    return cos_v, sin_v * u


def place_rows(k_ref, place_v):
    kx, ky = k_ref[0:1, :], k_ref[1:2, :]
    qx, qy = kx >= 0, ky >= 0
    mx, my = jnp.where(qx, kx, -1 - kx), jnp.where(qy, ky, -1 - ky)
    quad = 2 * qx.astype(jnp.int32) + qy.astype(jnp.int32)
    place_v[...] = ((quad * KMAX + mx) * KMAX + my) * 4


def spread_rows(s_ref, amp, abr, k_ref, grid_rows, x_even, x_odd, phase, place_v, place_s, sem, ready=(None,)):
    f32 = jnp.float32
    rows = s_ref.shape[0]
    place_rows(k_ref, place_v)
    idx_copy = pltpu.make_async_copy(place_v.at[0], place_s, sem)
    idx_copy.start()
    phase[0] = amp[...] * jnp.cos(abr[...])
    phase[1] = amp[...] * jnp.sin(abr[...])

    def turned(r, x_ref):
        here = pl.ds(pl.multiple_of(r * LANE, LANE), LANE)
        ph_c = jnp.broadcast_to(phase[0, pl.ds(r, 1), :], (LANE, LANE)).T
        ph_s = jnp.broadcast_to(phase[1, pl.ds(r, 1), :], (LANE, LANE)).T
        for h in range(2):
            re = s_ref[here, pl.ds(h * LANE, LANE)].astype(f32)
            im = s_ref[here, pl.ds((2 + h) * LANE, LANE)].astype(f32)
            x_ref[pl.ds(h, LANE, stride=4), :] = ph_c * re + ph_s * im
            x_ref[pl.ds(2 + h, LANE, stride=4), :] = ph_c * im - ph_s * re

    def scatter(r, x_ref):
        base = r * LANE
        for u in range(LANE):
            to = pl.multiple_of(place_s[base + u], 4)
            grid_rows[pl.ds(to, 4), :] = x_ref[4 * u : 4 * u + 4, :]

    part = rows // LANE // len(ready)
    for n, wait in enumerate(ready):
        first, last = n * part, (n + 1) * part - 1
        if wait is not None:
            wait()
        turned(first, x_even)
        if n == 0:
            idx_copy.wait()

        @pl.loop(first // 2, (last + 1) // 2)
        def _(i):
            r = 2 * i
            turned(r + 1, x_odd)
            scatter(r, x_even)
            turned(jnp.minimum(r + 2, last), x_even)
            scatter(r + 1, x_odd)


def own_kernel(
    s_own, amp, abr, k_ref, grid_rows, s_vmem, amp_v, abr_v, k_v, x_even, x_odd, phase, place_v, place_s, sem, sems
):
    rows = s_vmem.shape[0]
    chunks = [pl.ds(n * (rows // 2), rows // 2) for n in range(2)]
    pairs = [(k_ref, k_v), (amp, amp_v), (abr, abr_v)] + [(s_own.at[c], s_vmem.at[c]) for c in chunks]
    copies = [pltpu.make_async_copy(src, dst, sems.at[n]) for n, (src, dst) in enumerate(pairs)]
    for c in copies:
        c.start()
    for c in copies[:3]:
        c.wait()
    ready = [c.wait for c in copies[3:]]
    spread_rows(s_vmem, amp_v, abr_v, k_v, grid_rows, x_even, x_odd, phase, place_v, place_s, sem, ready)


def other_kernel(
    held, s_rem, amp, abr, k_ref, grid_rows, basis, x_even, x_odd, phase, place_v, place_s, sem
):
    bf16 = jnp.bfloat16
    spread_rows(s_rem, amp, abr, k_ref, grid_rows, x_even, x_odd, phase, place_v, place_s, sem)
    quarter = KMAX * KMAX * 4

    @pl.loop(0, KMAX * KMAX // LANE)
    def _(g):
        to = lambda n: pl.ds(pl.multiple_of((4 * g + n) * LANE, LANE), LANE)
        for h in range(2):
            vals = []
            for part in range(2):
                mm, mp, pm, pp = (
                    grid_rows[pl.ds(q * quarter + g * 4 * LANE + 2 * part + h, LANE, stride=4), :] for q in range(4)
                )
                a, b, c, d = pp + mm, pp - mm, pm + mp, pm - mp
                vals.append((a + c, c - a, b + d, b - d))
            re, im = vals
            at_re, at_im = pl.ds(2 * h * LANE, LANE), pl.ds((2 * h + 1) * LANE, LANE)
            for n in range(4):
                if n < 2:
                    basis[to(n), at_re], basis[to(n), at_im] = re[n].astype(bf16), im[n].astype(bf16)
                else:
                    basis[to(n), at_re], basis[to(n), at_im] = im[n].astype(bf16), (-re[n]).astype(bf16)


def waves(source, basis, coef_even, coef_odd, tab, emit):
    f32, bf16 = jnp.float32, jnp.bfloat16
    half = lax.axis_index("beam")
    blocks, step = source.shape[0], coef_even.shape[0]
    per = step // LANE

    def tables(j):
        pos = source[j, 8:10, :].astype(f32).astype(jnp.int32)
        width = pos.shape[1] // 2
        pos = 32 * pos[:, :width] + pos[:, width:]
        pos = jnp.where(half == 0, pos[:, :LANE], pos[:, LANE:])
        px, py = pos[0:1], pos[1:2]
        my = lax.broadcasted_iota(jnp.int32, (KMAX, LANE), 0)
        mx = lax.broadcasted_iota(jnp.int32, (8, LANE), 0)
        cy, sy = half_turns((2 * my + 1) * py)
        cx, sx = half_turns(jnp.where(mx < 4, 2 * mx + 1, 8) * px)
        reps = LANE // KMAX
        spread = lambda t: jnp.concatenate([jnp.broadcast_to(t[m : m + 1], (KMAX, LANE)) for m in range(reps)], 0)
        made = (
            jnp.concatenate([cy] * reps, 0), jnp.concatenate([sy] * reps, 0), spread(cx), spread(sx),
            jnp.broadcast_to(cx[4:5], (LANE, LANE)), jnp.broadcast_to(sx[4:5], (LANE, LANE)),
        )
        for n, t in enumerate(made):
            tab[n, j * LANE : (j + 1) * LANE, :] = t.T

    def coefficients(m, coef, sub=32):
        for row in range(0, step, sub):
            cy, sy, cx, sx, c4, s4 = (tab[n, m * step + row : m * step + row + sub, :] for n in range(6))
            for g in range(KMAX // 4):
                prods = (cx * cy, sx * sy, sx * cy, cx * sy)
                for n, v in enumerate(prods):
                    coef[row : row + sub, (4 * g + n) * LANE : (4 * g + n + 1) * LANE] = v.astype(bf16)
                cx, sx = cx * c4 - sx * s4, sx * c4 + cx * s4

    def prepare(m, coef):
        for j in range(m * per, (m + 1) * per):
            tables(j)
        coefficients(m, coef)

    prepare(0, coef_even)
    steps = blocks // per
    for m in range(steps):
        now, later = (coef_even, coef_odd) if m % 2 == 0 else (coef_odd, coef_even)
        psi = jnp.dot(now[...], basis[...], preferred_element_type=f32)
        if m + 1 < steps:
            prepare(m + 1, later)
        emit(m, psi)


def near_kernel(basis, near, psi_near, coef_even, coef_odd, tab):
    step = coef_even.shape[0]

    def emit(m, psi):
        psi_near[m * step : (m + 1) * step, :] = psi

    waves(near, basis, coef_even, coef_odd, tab, emit)


def far_kernel(basis, psi_near, near, far, cols, overlap, out, coef_even, coef_odd, tab, pots):
    f32, bf16 = jnp.float32, jnp.bfloat16
    column = lax.axis_index("probe")
    step = coef_even.shape[0]
    blocks = near.shape[0]
    for n, source in enumerate((near, far)):
        for j in range(blocks):
            owner = column ^ (n * blocks + j)
            pots[pl.ds(pl.multiple_of(owner * 8, 8), 8), :] = source[j, 0:8, :].astype(f32)
    mine = (cols[...] == column).astype(f32)
    left = (pots[...].T * mine).astype(bf16)
    right = pots[...].astype(bf16)
    g_re, g_im = overlap[0], overlap[1]
    mul = lambda a, b: jnp.dot(a, b, preferred_element_type=f32)
    forms = []
    for h in range(2):
        lr, li = left[h * LANE : (h + 1) * LANE], left[(2 + h) * LANE : (3 + h) * LANE]
        rr, ri = right[:, h * LANE : (h + 1) * LANE], right[:, (2 + h) * LANE : (3 + h) * LANE]
        r_re, r_im = mul(lr, rr) + mul(li, ri), mul(li, rr) - mul(lr, ri)
        h_re, h_im = g_re * r_re - g_im * r_im, g_re * r_im + g_im * r_re
        forms.append(
            jnp.concatenate([jnp.concatenate([h_re, h_im], 1), jnp.concatenate([-h_im, h_re], 1)], 0).astype(bf16)
        )

    def energy(first, psi):
        e = 0.0
        for h in range(2):
            wave = psi[:, 2 * h * LANE : (2 * h + 2) * LANE]
            v = wave * mul(wave.astype(bf16), forms[h])
            e = e + v[:, :LANE] + v[:, LANE:]
        for i in range(step // LANE):
            out[pl.ds(column ^ (first + i), 1), :] = jnp.sum(e[i * LANE : (i + 1) * LANE].T, axis=0, keepdims=True)

    def emit(m, psi):
        energy(blocks + m * step // LANE, psi)
        energy(m * step // LANE, psi_near[m * step : (m + 1) * step, :])

    waves(far, basis, coef_even, coef_odd, tab, emit)


def shards(smatrix, aperture, aberration, beam_k, probe_pos, patches, patch_col):
    f32, bf16 = jnp.float32, jnp.bfloat16
    blocks = lax.axis_size("probe")
    rows, width = smatrix.shape[0], smatrix.shape[2]
    swap = lambda v: lax.ppermute(v, "beam", [(0, 1), (1, 0)])
    s_own = smatrix.reshape(rows, width)
    s_rem = swap(s_own)
    amp_rem, abr_rem, k_rem = swap(aperture), swap(aberration), swap(beam_k)
    pos = jnp.concatenate([probe_pos // 32, probe_pos % 32], 1).astype(bf16)
    small = jnp.concatenate([patches, pos, jnp.zeros((6, width), bf16)], 0)[None]
    reach = 1
    while reach < blocks:
        far = lax.ppermute(small, "probe", [(i, i ^ reach) for i in range(blocks)])
        near, reach = small, 2 * reach
        if reach < blocks:
            small = jnp.concatenate([near, far], 0)

    vmem = pl.BlockSpec(memory_space=pltpu.VMEM)
    params = pltpu.CompilerParams(vmem_limit_bytes=24 * 1024 * 1024)
    grid = 4 * KMAX * KMAX
    lines = rows // LANE
    turning = [
        pltpu.VMEM((4 * LANE, LANE), f32),
        pltpu.VMEM((4 * LANE, LANE), f32),
        pltpu.VMEM((2, lines, LANE), f32),
        pltpu.VMEM((1, rows), jnp.int32),
        pltpu.SMEM((rows,), jnp.int32),
        pltpu.SemaphoreType.DMA,
    ]
    tile = lambda v: v.reshape(lines, LANE)
    cost = lambda n: pl.CostEstimate(flops=n, bytes_accessed=4 * 2**20, transcendentals=0)
    held_shape = jax.ShapeDtypeStruct((4 * grid, LANE), f32)
    hbm = pl.BlockSpec(memory_space=pltpu.HBM)
    held = pl.pallas_call(
        own_kernel,
        out_shape=held_shape,
        in_specs=[hbm] * 4,
        out_specs=vmem,
        scratch_shapes=[
            pltpu.VMEM((rows, width), bf16),
            pltpu.VMEM((lines, LANE), f32),
            pltpu.VMEM((lines, LANE), f32),
            pltpu.VMEM((2, rows), jnp.int32),
        ]
        + turning
        + [pltpu.SemaphoreType.DMA((5,))],
        compiler_params=params,
        cost_estimate=cost(3 * 10**9),
    )(*(pltpu.with_memory_space_constraint(v, pltpu.HBM) for v in (s_own, tile(aperture), tile(aberration), beam_k)))
    _, basis = pl.pallas_call(
        other_kernel,
        out_shape=(held_shape, jax.ShapeDtypeStruct((grid, width), bf16)),
        in_specs=[vmem] * 5,
        out_specs=(vmem, vmem),
        scratch_shapes=turning,
        input_output_aliases={0: 0},
        compiler_params=params,
        cost_estimate=cost(4 * 10**9),
    )(held, s_rem, tile(amp_rem), tile(abr_rem), k_rem)
    probes = blocks // 2 * LANE
    working = [
        pltpu.VMEM((2 * LANE, grid), bf16),
        pltpu.VMEM((2 * LANE, grid), bf16),
        pltpu.VMEM((6, probes, LANE), f32),
    ]
    psi_near = pl.pallas_call(
        near_kernel,
        out_shape=jax.ShapeDtypeStruct((probes, width), f32),
        in_specs=[vmem] * 2,
        out_specs=vmem,
        scratch_shapes=working,
        compiler_params=params,
        cost_estimate=cost(4 * 10**9),
    )(basis, near)
    energy = pl.pallas_call(
        far_kernel,
        out_shape=jax.ShapeDtypeStruct((blocks, LANE), f32),
        in_specs=[vmem] * 6,
        out_specs=vmem,
        scratch_shapes=working + [pltpu.VMEM((patch_col.shape[0], width), f32)],
        compiler_params=params,
        cost_estimate=cost(4 * 10**9),
    )(basis, psi_near, near, far, patch_col.reshape(1, -1), jnp.asarray(mode_overlap()))
    return lax.all_to_all(energy, "probe", 0, 0, tiled=True)


def solution(mesh):
    placed = (
        P(("grp", "beam"), "probe", None),
        P("beam"),
        P("beam"),
        P(None, "beam"),
        P(None, "probe"),
        P(("grp", "probe"), None),
        P("grp"),
    )
    return jax.shard_map(
        shards, mesh=mesh, in_specs=placed, out_specs=P("grp", ("probe", "beam")), check_vma=False
    )
```

```python
import functools
import math

import jax
import jax.numpy as jnp
import numpy as np
from jax import lax
from jax.experimental import pallas as pl
from jax.experimental.pallas import tpu as pltpu
from jax.sharding import PartitionSpec as P

PSIDE = 16
GRID = 1024
KMAX = 32
LANE = 128


def mode_overlap():
    pix = np.arange(LANE)
    row, col = pix // PSIDE, pix % PSIDE
    dist = col[:, None] - col[None, :]
    freq = np.arange(PSIDE // 2) - PSIDE // 4
    angle = (2.0 * math.pi / PSIDE) * ((freq[:, None, None] * dist[None]) % PSIDE)
    same = (row[:, None] == row[None, :]).astype(np.float64) * PSIDE / float(PSIDE**2 * (PSIDE**2 // 2))
    return np.stack([np.cos(angle).sum(0) * same, -np.sin(angle).sum(0) * same]).astype(np.float32)


def half_turns(count):
    folded = jnp.bitwise_and(count + GRID, 2 * GRID - 1) - GRID
    u = folded.astype(jnp.float32) * (1.0 / GRID)
    u2 = u * u
    terms = 9
    c = [(-1.0) ** k * math.pi ** (2 * k) / math.factorial(2 * k) for k in range(terms)]
    s = [(-1.0) ** k * math.pi ** (2 * k + 1) / math.factorial(2 * k + 1) for k in range(terms)]
    cos_v, sin_v = jnp.full_like(u, c[-1]), jnp.full_like(u, s[-1])
    for k in range(terms - 2, -1, -1):
        cos_v = cos_v * u2 + c[k]
        sin_v = sin_v * u2 + s[k]
    return cos_v, sin_v * u


def pack_kernel(amp, abr, k_hbm, pos_hbm, patches, small, param, amp_v, abr_v, k_v, pos_v, pat_v, sems):
    f32, bf16 = jnp.float32, jnp.bfloat16
    pairs = [(amp, amp_v), (abr, abr_v), (k_hbm, k_v), (pos_hbm, pos_v), (patches, pat_v)]
    copies = [pltpu.make_async_copy(src, dst, sems.at[n]) for n, (src, dst) in enumerate(pairs)]
    for c in copies:
        c.start()
    for c in copies:
        c.wait()
    half = lax.axis_index("beam")
    pats = pat_v[...].astype(f32)
    pos = jnp.where(half == 0, pos_v[:, :LANE], pos_v[:, LANE:])
    tiles = [pats[:, t * LANE : (t + 1) * LANE] for t in range(pats.shape[1] // LANE)]
    split = [(pos // 32).astype(f32), (pos % 32).astype(f32), jnp.zeros((12, LANE), f32)]
    message = jnp.concatenate(tiles + [jnp.concatenate(split, 0)], 0)
    small[0] = message.astype(bf16)
    lines = amp_v.shape[0]
    param[0:lines, :] = amp_v[...] * jnp.cos(abr_v[...])
    param[lines : 2 * lines, :] = amp_v[...] * jnp.sin(abr_v[...])
    kx, ky = k_v[0:1, :], k_v[1:2, :]
    qx, qy = kx >= 0, ky >= 0
    mx, my = jnp.where(qx, kx, -1 - kx), jnp.where(qy, ky, -1 - ky)
    quad = 2 * qx.astype(jnp.int32) + qy.astype(jnp.int32)
    place = (((quad * KMAX + mx) * KMAX + my) * 4).astype(f32)
    for r in range(lines):
        param[2 * lines + r : 2 * lines + r + 1, :] = place[:, r * LANE : (r + 1) * LANE]


def spread_rows(s_ref, param, grid_rows, x_even, x_odd, place_v, place_s, sem, ready=()):
    f32 = jnp.float32
    lines = s_ref.shape[0] // LANE
    place = param[2 * lines : 3 * lines, :].astype(jnp.int32)
    for r in range(lines):
        place_v[0:1, r * LANE : (r + 1) * LANE] = place[r : r + 1, :]
    idx_copy = pltpu.make_async_copy(place_v.at[0], place_s, sem)
    idx_copy.start()

    def turned(r, x_ref):
        here = pl.ds(pl.multiple_of(r * LANE, LANE), LANE)
        ph_c = jnp.broadcast_to(param[pl.ds(r, 1), :], (LANE, LANE)).T
        ph_s = jnp.broadcast_to(param[pl.ds(lines + r, 1), :], (LANE, LANE)).T
        for h in range(2):
            re = s_ref[here, pl.ds(h * LANE, LANE)].astype(f32)
            im = s_ref[here, pl.ds((2 + h) * LANE, LANE)].astype(f32)
            x_ref[pl.ds(h, LANE, stride=4), :] = ph_c * re + ph_s * im
            x_ref[pl.ds(2 + h, LANE, stride=4), :] = ph_c * im - ph_s * re

    def scatter(r, x_ref):
        base = r * LANE
        for u in range(LANE):
            to = pl.multiple_of(place_s[base + u], 4)
            grid_rows[pl.ds(to, 4), :] = x_ref[4 * u : 4 * u + 4, :]

    stops = [last for last, _ in ready] + [lines] if ready else [0, lines]
    waits = [wait for _, wait in ready] if ready else [lambda: None]
    idx_copy.wait()
    for first, stop, wait in zip(stops, stops[1:], waits):
        wait()
        turned(first, x_even)

        @pl.loop(first // 2, stop // 2)
        def _(i):
            r = 2 * i
            turned(r + 1, x_odd)
            scatter(r, x_even)
            turned(jnp.minimum(r + 2, stop - 1), x_even)
            scatter(r + 1, x_odd)


def own_kernel(s_own, param, grid_rows, zero, s_vmem, sems, *scratch):
    lines = s_vmem.shape[0] // LANE
    starts = (0, lines // 4)
    ready = []
    for n, (first, stop) in enumerate(zip(starts, starts[1:] + (lines,))):
        part = pl.ds(first * LANE, (stop - first) * LANE)
        load = pltpu.make_async_copy(s_own.at[part], s_vmem.at[part], sems.at[n])
        load.start()
        ready.append((first, load.wait))
    zero[...] = jnp.zeros_like(zero)
    spread_rows(s_vmem, param, grid_rows, *scratch, ready=ready)


def other_kernel(held, s_rem, param, grid_rows, basis, zero, *scratch):
    bf16 = jnp.bfloat16
    zero[...] = jnp.zeros_like(zero)
    spread_rows(s_rem, param, grid_rows, *scratch)
    quarter = KMAX * KMAX * 4

    @pl.loop(0, KMAX * KMAX // LANE)
    def _(g):
        to = lambda n: pl.ds(pl.multiple_of((4 * g + n) * LANE, LANE), LANE)
        for h in range(2):
            vals = []
            for part in range(2):
                mm, mp, pm, pp = (
                    grid_rows[pl.ds(q * quarter + g * 4 * LANE + 2 * part + h, LANE, stride=4), :] for q in range(4)
                )
                a, b, c, d = pp + mm, pp - mm, pm + mp, pm - mp
                vals.append((a + c, c - a, b + d, b - d))
            re, im = vals
            at_re, at_im = pl.ds(2 * h * LANE, LANE), pl.ds((2 * h + 1) * LANE, LANE)
            for n in range(4):
                if n < 2:
                    basis[to(n), at_re], basis[to(n), at_im] = re[n].astype(bf16), im[n].astype(bf16)
                else:
                    basis[to(n), at_re], basis[to(n), at_im] = im[n].astype(bf16), (-re[n]).astype(bf16)


def waves(source, basis, coef_even, coef_odd, tab, emit):
    f32, bf16 = jnp.float32, jnp.bfloat16
    blocks, step = source.shape[0], coef_even.shape[0]
    per = step // LANE

    def tables(j):
        pos = source[j, 32:48, :].astype(f32).astype(jnp.int32)
        px, py = 32 * pos[0:1] + pos[2:3], 32 * pos[1:2] + pos[3:4]
        my = lax.broadcasted_iota(jnp.int32, (KMAX, LANE), 0)
        mx = lax.broadcasted_iota(jnp.int32, (8, LANE), 0)
        cy, sy = half_turns((2 * my + 1) * py)
        cx, sx = half_turns(jnp.where(mx < 4, 2 * mx + 1, 8) * px)
        reps = LANE // KMAX
        spread = lambda t: jnp.concatenate([jnp.broadcast_to(t[m : m + 1], (KMAX, LANE)) for m in range(reps)], 0)
        made = (
            jnp.concatenate([cy] * reps, 0), jnp.concatenate([sy] * reps, 0), spread(cx), spread(sx),
            jnp.broadcast_to(cx[4:5], (LANE, LANE)), jnp.broadcast_to(sx[4:5], (LANE, LANE)),
        )
        for n, t in enumerate(made):
            tab[n, j * LANE : (j + 1) * LANE, :] = t.T

    def coefficients(m, coef, sub=32):
        for row in range(0, step, sub):
            cy, sy, cx, sx, c4, s4 = (tab[n, m * step + row : m * step + row + sub, :] for n in range(6))
            for g in range(KMAX // 4):
                prods = (cx * cy, sx * sy, sx * cy, cx * sy)
                for n, v in enumerate(prods):
                    coef[row : row + sub, (4 * g + n) * LANE : (4 * g + n + 1) * LANE] = v.astype(bf16)
                cx, sx = cx * c4 - sx * s4, sx * c4 + cx * s4

    def prepare(m, coef):
        for j in range(m * per, (m + 1) * per):
            tables(j)
        coefficients(m, coef)

    prepare(0, coef_even)
    steps = blocks // per
    for m in range(steps):
        now, later = (coef_even, coef_odd) if m % 2 == 0 else (coef_odd, coef_even)
        psi = jnp.dot(now[...], basis[...], preferred_element_type=f32)
        if m + 1 < steps:
            prepare(m + 1, later)
        emit(m, psi)


def near_kernel(basis, near, psi_near, coef_even, coef_odd, tab):
    step = coef_even.shape[0]

    def emit(m, psi):
        psi_near[m * step : (m + 1) * step, :] = psi

    waves(near, basis, coef_even, coef_odd, tab, emit)


def far_kernel(masks, basis, psi_near, near, far, cols, overlap, out, coef_even, coef_odd, tab, pots):
    f32, bf16 = jnp.float32, jnp.bfloat16
    column = lax.axis_index("probe")
    step = coef_even.shape[0]
    blocks = near.shape[0]
    for n, source in enumerate((near, far)):
        for j in range(blocks):
            owner = column ^ masks[n * blocks + j]
            pats = source[j, 0:32, :].astype(f32)
            for t in range(4):
                pots[pl.ds(pl.multiple_of(owner * 8, 8), 8), t * LANE : (t + 1) * LANE] = pats[8 * t : 8 * t + 8]
    mine = (cols[...] == column).astype(f32)
    left = (pots[...].T * mine).astype(bf16)
    right = pots[...].astype(bf16)
    g_re, g_im = overlap[0], overlap[1]
    mul = lambda a, b: jnp.dot(a, b, preferred_element_type=f32)
    forms = []
    for h in range(2):
        lr, li = left[h * LANE : (h + 1) * LANE], left[(2 + h) * LANE : (3 + h) * LANE]
        rr, ri = right[:, h * LANE : (h + 1) * LANE], right[:, (2 + h) * LANE : (3 + h) * LANE]
        r_re, r_im = mul(lr, rr) + mul(li, ri), mul(li, rr) - mul(lr, ri)
        h_re, h_im = g_re * r_re - g_im * r_im, g_re * r_im + g_im * r_re
        forms.append(
            jnp.concatenate([jnp.concatenate([h_re, h_im], 1), jnp.concatenate([-h_im, h_re], 1)], 0).astype(bf16)
        )

    def energy(first, psi):
        e = 0.0
        for h in range(2):
            wave = psi[:, 2 * h * LANE : (2 * h + 2) * LANE]
            v = wave * mul(wave.astype(bf16), forms[h])
            e = e + v[:, :LANE] + v[:, LANE:]
        for i in range(step // LANE):
            out[pl.ds(column ^ masks[first + i], 1), :] = jnp.sum(e[i * LANE : (i + 1) * LANE].T, axis=0, keepdims=True)

    def emit(m, psi):
        energy(blocks + m * step // LANE, psi)
        energy(m * step // LANE, psi_near[m * step : (m + 1) * step, :])

    waves(far, basis, coef_even, coef_odd, tab, emit)


def shards(smatrix, aperture, aberration, beam_k, probe_pos, patches, patch_col):
    f32, bf16 = jnp.float32, jnp.bfloat16
    blocks = lax.axis_size("probe")
    rows, width = smatrix.shape[0], smatrix.shape[2]
    lines, grid = rows // LANE, 4 * KMAX * KMAX
    swap = lambda v: lax.ppermute(v, "beam", [(0, 1), (1, 0)])
    sds = jax.ShapeDtypeStruct
    vmem, hbm = pl.BlockSpec(memory_space=pltpu.VMEM), pl.BlockSpec(memory_space=pltpu.HBM)
    params = pltpu.CompilerParams(vmem_limit_bytes=24 * 1024 * 1024)
    cost = lambda n: pl.CostEstimate(flops=n, bytes_accessed=4 * 2**20, transcendentals=0)

    message = sds((1, 48, LANE), bf16)
    s_own = smatrix.reshape(rows, width)
    raw = (aperture.reshape(lines, LANE), aberration.reshape(lines, LANE), beam_k, probe_pos, patches)
    small, param = pl.pallas_call(
        pack_kernel,
        out_shape=(message, sds((3 * lines, LANE), f32)),
        in_specs=[hbm] * len(raw),
        out_specs=(vmem,) * 2,
        scratch_shapes=[pltpu.VMEM(v.shape, v.dtype) for v in raw] + [pltpu.SemaphoreType.DMA((len(raw),))],
        compiler_params=params,
        cost_estimate=cost(10**9),
    )(*(pltpu.with_memory_space_constraint(v, pltpu.HBM) for v in raw))
    param_rem = swap(param)
    later, _ = lax.optimization_barrier((s_own, small))
    s_rem = swap(later)

    turning = [
        pltpu.VMEM((4 * LANE, LANE), f32),
        pltpu.VMEM((4 * LANE, LANE), f32),
        pltpu.VMEM((1, rows), jnp.int32),
        pltpu.SMEM((rows,), jnp.int32),
        pltpu.SemaphoreType.DMA,
    ]
    held_shape = sds((4 * grid, LANE), f32)
    held, zero_own = pl.pallas_call(
        own_kernel,
        out_shape=(held_shape, message),
        in_specs=[hbm, vmem],
        out_specs=(vmem,) * 2,
        scratch_shapes=[pltpu.VMEM((rows, width), bf16), pltpu.SemaphoreType.DMA((2,))] + turning,
        compiler_params=params,
        cost_estimate=cost(3 * 10**9),
    )(pltpu.with_memory_space_constraint(s_own, pltpu.HBM), param)
    _, basis, zero_other = pl.pallas_call(
        other_kernel,
        out_shape=(held_shape, sds((grid, width), bf16), message),
        in_specs=[vmem] * 3,
        out_specs=(vmem,) * 3,
        scratch_shapes=turning,
        input_output_aliases={0: 0},
        compiler_params=params,
        cost_estimate=cost(4 * 10**9),
    )(held, s_rem, param_rem)

    steps = [1 << n for n in range(blocks.bit_length() - 1)]
    steps = steps[-2:] + steps[:-2][::-1]
    beside, masks = [zero_own, zero_other], [0]
    for reach in steps:
        far = lax.ppermute(small, "probe", [(i, i ^ reach) for i in range(blocks)])
        masks = masks + [m ^ reach for m in masks]
        near = small
        if reach != steps[-1]:
            small = jnp.concatenate([near, far + beside.pop(0) if beside else far], 0)

    probes = blocks // 2 * LANE
    working = [
        pltpu.VMEM((2 * LANE, grid), bf16),
        pltpu.VMEM((2 * LANE, grid), bf16),
        pltpu.VMEM((6, probes, LANE), f32),
    ]
    psi_near = pl.pallas_call(
        near_kernel,
        out_shape=jax.ShapeDtypeStruct((probes, width), f32),
        in_specs=[vmem] * 2,
        out_specs=vmem,
        scratch_shapes=working,
        compiler_params=params,
        cost_estimate=cost(4 * 10**9),
    )(basis, near)
    energy = pl.pallas_call(
        functools.partial(far_kernel, tuple(masks)),
        out_shape=jax.ShapeDtypeStruct((blocks, LANE), f32),
        in_specs=[vmem] * 6,
        out_specs=vmem,
        scratch_shapes=working + [pltpu.VMEM((patch_col.shape[0], width), f32)],
        compiler_params=params,
        cost_estimate=cost(4 * 10**9),
    )(basis, psi_near, near, far, patch_col.reshape(1, -1), jnp.asarray(mode_overlap()))
    return lax.all_to_all(energy, "probe", 0, 0, tiled=True)


def solution(mesh):
    placed = (
        P(("grp", "beam"), "probe", None),
        P("beam"),
        P("beam"),
        P(None, "beam"),
        P(None, "probe"),
        P(("grp", "probe"), None),
        P("grp"),
    )
    return jax.shard_map(
        shards, mesh=mesh, in_specs=placed, out_specs=P("grp", ("probe", "beam")), check_vma=False
    )
```

```python
import functools
import math

import jax
import jax.numpy as jnp
import numpy as np
from jax import lax
from jax.experimental import pallas as pl
from jax.experimental.pallas import tpu as pltpu
from jax.sharding import PartitionSpec as P

PSIDE = 16
GRID = 1024
KMAX = 32
LANE = 128


def mode_overlap():
    pix = np.arange(LANE)
    row, col = pix // PSIDE, pix % PSIDE
    dist = col[:, None] - col[None, :]
    freq = np.arange(PSIDE // 2) - PSIDE // 4
    angle = (2.0 * math.pi / PSIDE) * ((freq[:, None, None] * dist[None]) % PSIDE)
    same = (row[:, None] == row[None, :]).astype(np.float64) * PSIDE / float(PSIDE**2 * (PSIDE**2 // 2))
    return np.stack([np.cos(angle).sum(0) * same, -np.sin(angle).sum(0) * same]).astype(np.float32)


def half_turns(count):
    folded = jnp.bitwise_and(count + GRID, 2 * GRID - 1) - GRID
    u = folded.astype(jnp.float32) * (1.0 / GRID)
    u2 = u * u
    terms = 9
    c = [(-1.0) ** k * math.pi ** (2 * k) / math.factorial(2 * k) for k in range(terms)]
    s = [(-1.0) ** k * math.pi ** (2 * k + 1) / math.factorial(2 * k + 1) for k in range(terms)]
    cos_v, sin_v = jnp.full_like(u, c[-1]), jnp.full_like(u, s[-1])
    for k in range(terms - 2, -1, -1):
        cos_v = cos_v * u2 + c[k]
        sin_v = sin_v * u2 + s[k]
    return cos_v, sin_v * u


def pack_kernel(amp, abr, k_hbm, pos_hbm, patches, small, param, amp_v, abr_v, k_v, pos_v, pat_v, sems):
    f32, bf16 = jnp.float32, jnp.bfloat16
    pairs = [(amp, amp_v), (abr, abr_v), (k_hbm, k_v), (pos_hbm, pos_v), (patches, pat_v)]
    copies = [pltpu.make_async_copy(src, dst, sems.at[n]) for n, (src, dst) in enumerate(pairs)]
    for c in copies:
        c.start()
    for c in copies:
        c.wait()
    pats = pat_v[...].astype(f32)
    pos = jnp.concatenate([pos_v[:, :LANE], pos_v[:, LANE:]], 0)
    tiles = [pats[:, t * LANE : (t + 1) * LANE] for t in range(pats.shape[1] // LANE)]
    split = [(pos // 32).astype(f32), (pos % 32).astype(f32), jnp.zeros((8, LANE), f32)]
    message = jnp.concatenate(tiles + [jnp.concatenate(split, 0)], 0)
    small[0] = message.astype(bf16)
    lines = amp_v.shape[0]
    param[0:lines, :] = amp_v[...] * jnp.cos(abr_v[...])
    param[lines : 2 * lines, :] = amp_v[...] * jnp.sin(abr_v[...])
    kx, ky = k_v[0:1, :], k_v[1:2, :]
    qx, qy = kx >= 0, ky >= 0
    mx, my = jnp.where(qx, kx, -1 - kx), jnp.where(qy, ky, -1 - ky)
    quad = 2 * qx.astype(jnp.int32) + qy.astype(jnp.int32)
    place = (((quad * KMAX + mx) * KMAX + my) * 4).astype(f32)
    for r in range(lines):
        param[2 * lines + r : 2 * lines + r + 1, :] = place[:, r * LANE : (r + 1) * LANE]


def spread_rows(s_ref, param, grid_rows, x_even, x_odd, place_v, place_s, sem, ready=()):
    f32 = jnp.float32
    lines = s_ref.shape[0] // LANE
    place = param[2 * lines : 3 * lines, :].astype(jnp.int32)
    for r in range(lines):
        place_v[0:1, r * LANE : (r + 1) * LANE] = place[r : r + 1, :]
    idx_copy = pltpu.make_async_copy(place_v.at[0], place_s, sem)
    idx_copy.start()

    def turned(r, x_ref):
        here = pl.ds(pl.multiple_of(r * LANE, LANE), LANE)
        ph_c = jnp.broadcast_to(param[pl.ds(r, 1), :], (LANE, LANE)).T
        ph_s = jnp.broadcast_to(param[pl.ds(lines + r, 1), :], (LANE, LANE)).T
        for h in range(2):
            re = s_ref[here, pl.ds(h * LANE, LANE)].astype(f32)
            im = s_ref[here, pl.ds((2 + h) * LANE, LANE)].astype(f32)
            x_ref[pl.ds(h, LANE, stride=4), :] = ph_c * re + ph_s * im
            x_ref[pl.ds(2 + h, LANE, stride=4), :] = ph_c * im - ph_s * re

    def scatter(r, x_ref):
        base = r * LANE
        for u in range(LANE):
            to = pl.multiple_of(place_s[base + u], 4)
            grid_rows[pl.ds(to, 4), :] = x_ref[4 * u : 4 * u + 4, :]

    stops = [last for last, _ in ready] + [lines] if ready else [0, lines]
    waits = [wait for _, wait in ready] if ready else [lambda: None]
    idx_copy.wait()
    for first, stop, wait in zip(stops, stops[1:], waits):
        wait()
        turned(first, x_even)

        @pl.loop(first // 2, stop // 2)
        def _(i):
            r = 2 * i
            turned(r + 1, x_odd)
            scatter(r, x_even)
            turned(jnp.minimum(r + 2, stop - 1), x_even)
            scatter(r + 1, x_odd)


def own_kernel(s_own, param, grid_rows, zero, s_vmem, sems, *scratch):
    lines = s_vmem.shape[0] // LANE
    starts = (0, lines // 4)
    ready = []
    for n, (first, stop) in enumerate(zip(starts, starts[1:] + (lines,))):
        part = pl.ds(first * LANE, (stop - first) * LANE)
        load = pltpu.make_async_copy(s_own.at[part], s_vmem.at[part], sems.at[n])
        load.start()
        ready.append((first, load.wait))
    zero[...] = jnp.zeros_like(zero)
    spread_rows(s_vmem, param, grid_rows, *scratch, ready=ready)


def other_kernel(held, s_rem, param, grid_rows, basis, zero, *scratch):
    bf16 = jnp.bfloat16
    zero[...] = jnp.zeros_like(zero)
    spread_rows(s_rem, param, grid_rows, *scratch)
    quarter = KMAX * KMAX * 4

    @pl.loop(0, KMAX * KMAX // LANE)
    def _(g):
        to = lambda n: pl.ds(pl.multiple_of((4 * g + n) * LANE, LANE), LANE)
        for h in range(2):
            vals = []
            for part in range(2):
                mm, mp, pm, pp = (
                    grid_rows[pl.ds(q * quarter + g * 4 * LANE + 2 * part + h, LANE, stride=4), :] for q in range(4)
                )
                a, b, c, d = pp + mm, pp - mm, pm + mp, pm - mp
                vals.append((a + c, c - a, b + d, b - d))
            re, im = vals
            at_re, at_im = pl.ds(2 * h * LANE, LANE), pl.ds((2 * h + 1) * LANE, LANE)
            for n in range(4):
                if n < 2:
                    basis[to(n), at_re], basis[to(n), at_im] = re[n].astype(bf16), im[n].astype(bf16)
                else:
                    basis[to(n), at_re], basis[to(n), at_im] = im[n].astype(bf16), (-re[n]).astype(bf16)


def waves(source, basis, coef_even, coef_odd, tab, emit):
    f32, bf16 = jnp.float32, jnp.bfloat16
    half = lax.axis_index("beam")
    blocks, step = source.shape[0], coef_even.shape[0]
    per = step // LANE

    def tables(j):
        pos = source[j, 32:48, :].astype(f32).astype(jnp.int32)
        pos = 32 * pos[0:4] + pos[4:8]
        pos = jnp.where(half == 0, pos[0:2], pos[2:4])
        px, py = pos[0:1], pos[1:2]
        my = lax.broadcasted_iota(jnp.int32, (KMAX, LANE), 0)
        mx = lax.broadcasted_iota(jnp.int32, (8, LANE), 0)
        cy, sy = half_turns((2 * my + 1) * py)
        cx, sx = half_turns(jnp.where(mx < 4, 2 * mx + 1, 8) * px)
        reps = LANE // KMAX
        spread = lambda t: jnp.concatenate([jnp.broadcast_to(t[m : m + 1], (KMAX, LANE)) for m in range(reps)], 0)
        made = (
            jnp.concatenate([cy] * reps, 0), jnp.concatenate([sy] * reps, 0), spread(cx), spread(sx),
            jnp.broadcast_to(cx[4:5], (LANE, LANE)), jnp.broadcast_to(sx[4:5], (LANE, LANE)),
        )
        for n, t in enumerate(made):
            tab[n, j * LANE : (j + 1) * LANE, :] = t.T

    def coefficients(m, coef, sub=32):
        for row in range(0, step, sub):
            cy, sy, cx, sx, c4, s4 = (tab[n, m * step + row : m * step + row + sub, :] for n in range(6))
            for g in range(KMAX // 4):
                prods = (cx * cy, sx * sy, sx * cy, cx * sy)
                for n, v in enumerate(prods):
                    coef[row : row + sub, (4 * g + n) * LANE : (4 * g + n + 1) * LANE] = v.astype(bf16)
                cx, sx = cx * c4 - sx * s4, sx * c4 + cx * s4

    def prepare(m, coef):
        for j in range(m * per, (m + 1) * per):
            tables(j)
        coefficients(m, coef)

    prepare(0, coef_even)
    steps = blocks // per
    for m in range(steps):
        now, later = (coef_even, coef_odd) if m % 2 == 0 else (coef_odd, coef_even)
        psi = jnp.dot(now[...], basis[...], preferred_element_type=f32)
        if m + 1 < steps:
            prepare(m + 1, later)
        emit(m, psi)


def near_kernel(basis, near, psi_near, coef_even, coef_odd, tab):
    step = coef_even.shape[0]

    def emit(m, psi):
        psi_near[m * step : (m + 1) * step, :] = psi

    waves(near, basis, coef_even, coef_odd, tab, emit)


def far_kernel(masks, basis, psi_near, near, far, cols, overlap, out, coef_even, coef_odd, tab, pots):
    f32, bf16 = jnp.float32, jnp.bfloat16
    column = lax.axis_index("probe")
    step = coef_even.shape[0]
    blocks = near.shape[0]
    for n, source in enumerate((near, far)):
        for j in range(blocks):
            owner = column ^ masks[n * blocks + j]
            pats = source[j, 0:32, :].astype(f32)
            for t in range(4):
                pots[pl.ds(pl.multiple_of(owner * 8, 8), 8), t * LANE : (t + 1) * LANE] = pats[8 * t : 8 * t + 8]
    mine = (cols[...] == column).astype(f32)
    left = (pots[...].T * mine).astype(bf16)
    right = pots[...].astype(bf16)
    g_re, g_im = overlap[0], overlap[1]
    mul = lambda a, b: jnp.dot(a, b, preferred_element_type=f32)
    forms = []
    for h in range(2):
        lr, li = left[h * LANE : (h + 1) * LANE], left[(2 + h) * LANE : (3 + h) * LANE]
        rr, ri = right[:, h * LANE : (h + 1) * LANE], right[:, (2 + h) * LANE : (3 + h) * LANE]
        r_re, r_im = mul(lr, rr) + mul(li, ri), mul(li, rr) - mul(lr, ri)
        h_re, h_im = g_re * r_re - g_im * r_im, g_re * r_im + g_im * r_re
        forms.append(
            jnp.concatenate([jnp.concatenate([h_re, h_im], 1), jnp.concatenate([-h_im, h_re], 1)], 0).astype(bf16)
        )

    def energy(first, psi):
        e = 0.0
        for h in range(2):
            wave = psi[:, 2 * h * LANE : (2 * h + 2) * LANE]
            v = wave * mul(wave.astype(bf16), forms[h])
            e = e + v[:, :LANE] + v[:, LANE:]
        for i in range(step // LANE):
            out[pl.ds(column ^ masks[first + i], 1), :] = jnp.sum(e[i * LANE : (i + 1) * LANE].T, axis=0, keepdims=True)

    def emit(m, psi):
        energy(blocks + m * step // LANE, psi)
        energy(m * step // LANE, psi_near[m * step : (m + 1) * step, :])

    waves(far, basis, coef_even, coef_odd, tab, emit)


def shards(smatrix, aperture, aberration, beam_k, probe_pos, patches, patch_col):
    f32, bf16 = jnp.float32, jnp.bfloat16
    blocks = lax.axis_size("probe")
    rows, width = smatrix.shape[0], smatrix.shape[2]
    lines, grid = rows // LANE, 4 * KMAX * KMAX
    swap = lambda v: lax.ppermute(v, "beam", [(0, 1), (1, 0)])
    sds = jax.ShapeDtypeStruct
    vmem, hbm = pl.BlockSpec(memory_space=pltpu.VMEM), pl.BlockSpec(memory_space=pltpu.HBM)
    params = pltpu.CompilerParams(vmem_limit_bytes=24 * 1024 * 1024)
    cost = lambda n: pl.CostEstimate(flops=n, bytes_accessed=4 * 2**20, transcendentals=0)

    message = sds((1, 48, LANE), bf16)
    s_own = smatrix.reshape(rows, width)
    raw = (aperture.reshape(lines, LANE), aberration.reshape(lines, LANE), beam_k, probe_pos, patches)
    small, param = pl.pallas_call(
        pack_kernel,
        out_shape=(message, sds((3 * lines, LANE), f32)),
        in_specs=[hbm] * len(raw),
        out_specs=(vmem,) * 2,
        scratch_shapes=[pltpu.VMEM(v.shape, v.dtype) for v in raw] + [pltpu.SemaphoreType.DMA((len(raw),))],
        compiler_params=params,
        cost_estimate=cost(10**9),
    )(*(pltpu.with_memory_space_constraint(v, pltpu.HBM) for v in raw))
    param_rem = swap(param)
    later, _ = lax.optimization_barrier((s_own, small))
    s_rem = swap(later)

    turning = [
        pltpu.VMEM((4 * LANE, LANE), f32),
        pltpu.VMEM((4 * LANE, LANE), f32),
        pltpu.VMEM((1, rows), jnp.int32),
        pltpu.SMEM((rows,), jnp.int32),
        pltpu.SemaphoreType.DMA,
    ]
    held_shape = sds((4 * grid + 24, LANE), f32)
    held, zero_own = pl.pallas_call(
        own_kernel,
        out_shape=(held_shape, message),
        in_specs=[hbm, vmem],
        out_specs=(vmem,) * 2,
        scratch_shapes=[pltpu.VMEM((rows, width), bf16), pltpu.SemaphoreType.DMA((2,))] + turning,
        compiler_params=params,
        cost_estimate=cost(3 * 10**9),
    )(pltpu.with_memory_space_constraint(s_own, pltpu.HBM), param)
    _, basis, zero_other = pl.pallas_call(
        other_kernel,
        out_shape=(held_shape, sds((grid, width), bf16), message),
        in_specs=[vmem] * 3,
        out_specs=(vmem,) * 3,
        scratch_shapes=turning,
        input_output_aliases={0: 0},
        compiler_params=params,
        cost_estimate=cost(4 * 10**9),
    )(held, s_rem, param_rem)

    steps = [1 << n for n in range(blocks.bit_length() - 1)]
    steps = steps[-2:] + steps[:-2][::-1]
    beside, masks = [zero_own, zero_other], [0]
    for reach in steps:
        far = lax.ppermute(
            small, ("probe", "beam"), [(2 * i + b, 2 * (i ^ reach) + 1 - b) for i in range(blocks) for b in range(2)]
        )
        masks = masks + [m ^ reach for m in masks]
        near = small
        if reach != steps[-1]:
            small = jnp.concatenate([near, far + beside.pop(0) if beside else far], 0)

    probes = blocks // 2 * LANE
    working = [
        pltpu.VMEM((2 * LANE, grid), bf16),
        pltpu.VMEM((2 * LANE, grid), bf16),
        pltpu.VMEM((6, probes, LANE), f32),
    ]
    psi_near = pl.pallas_call(
        near_kernel,
        out_shape=jax.ShapeDtypeStruct((probes, width), f32),
        in_specs=[vmem] * 2,
        out_specs=vmem,
        scratch_shapes=working,
        compiler_params=params,
        cost_estimate=cost(4 * 10**9),
    )(basis, near)
    energy = pl.pallas_call(
        functools.partial(far_kernel, tuple(masks)),
        out_shape=jax.ShapeDtypeStruct((blocks, LANE), f32),
        in_specs=[vmem] * 6,
        out_specs=vmem,
        scratch_shapes=working + [pltpu.VMEM((patch_col.shape[0], width), f32)],
        compiler_params=params,
        cost_estimate=cost(4 * 10**9),
    )(basis, psi_near, near, far, patch_col.reshape(1, -1), jnp.asarray(mode_overlap()))
    return lax.all_to_all(energy, "probe", 0, 0, tiled=True)


def solution(mesh):
    placed = (
        P(("grp", "beam"), "probe", None),
        P("beam"),
        P("beam"),
        P(None, "beam"),
        P(None, "probe"),
        P(("grp", "probe"), None),
        P("grp"),
    )
    return jax.shard_map(
        shards, mesh=mesh, in_specs=placed, out_specs=P("grp", ("probe", "beam")), check_vma=False
    )
```

```python
import functools
import math

import jax
import jax.numpy as jnp
import numpy as np
from jax import lax
from jax.experimental import pallas as pl
from jax.experimental.pallas import tpu as pltpu
from jax.sharding import PartitionSpec as P

PSIDE = 16
GRID = 1024
KMAX = 32
LANE = 128


def mode_overlap():
    pix = np.arange(LANE)
    row, col = pix // PSIDE, pix % PSIDE
    dist = col[:, None] - col[None, :]
    freq = np.arange(PSIDE // 2) - PSIDE // 4
    angle = (2.0 * math.pi / PSIDE) * ((freq[:, None, None] * dist[None]) % PSIDE)
    same = (row[:, None] == row[None, :]).astype(np.float64) * PSIDE / float(PSIDE**2 * (PSIDE**2 // 2))
    return np.stack([np.cos(angle).sum(0) * same, -np.sin(angle).sum(0) * same]).astype(np.float32)


def half_turns(count):
    folded = jnp.bitwise_and(count + GRID, 2 * GRID - 1) - GRID
    u = folded.astype(jnp.float32) * (1.0 / GRID)
    u2 = u * u
    terms = 9
    c = [(-1.0) ** k * math.pi ** (2 * k) / math.factorial(2 * k) for k in range(terms)]
    s = [(-1.0) ** k * math.pi ** (2 * k + 1) / math.factorial(2 * k + 1) for k in range(terms)]
    cos_v, sin_v = jnp.full_like(u, c[-1]), jnp.full_like(u, s[-1])
    for k in range(terms - 2, -1, -1):
        cos_v = cos_v * u2 + c[k]
        sin_v = sin_v * u2 + s[k]
    return cos_v, sin_v * u


def pack_kernel(amp, abr, k_hbm, pos_hbm, patches, small, param, amp_v, abr_v, k_v, pos_v, pat_v, sems):
    f32, bf16 = jnp.float32, jnp.bfloat16
    pairs = [(amp, amp_v), (abr, abr_v), (k_hbm, k_v), (pos_hbm, pos_v), (patches, pat_v)]
    copies = [pltpu.make_async_copy(src, dst, sems.at[n]) for n, (src, dst) in enumerate(pairs)]
    for c in copies:
        c.start()
    for c in copies:
        c.wait()
    pats = pat_v[...].astype(f32)
    pos = jnp.concatenate([pos_v[:, :LANE], pos_v[:, LANE:]], 0)
    tiles = [pats[:, t * LANE : (t + 1) * LANE] for t in range(pats.shape[1] // LANE)]
    split = [(pos // 32).astype(f32), (pos % 32).astype(f32), jnp.zeros((8, LANE), f32)]
    message = jnp.concatenate(tiles + [jnp.concatenate(split, 0)], 0)
    small[0] = message.astype(bf16)
    lines = amp_v.shape[0]
    param[0:lines, :] = amp_v[...] * jnp.cos(abr_v[...])
    param[lines : 2 * lines, :] = amp_v[...] * jnp.sin(abr_v[...])
    kx, ky = k_v[0:1, :], k_v[1:2, :]
    qx, qy = kx >= 0, ky >= 0
    mx, my = jnp.where(qx, kx, -1 - kx), jnp.where(qy, ky, -1 - ky)
    quad = 2 * qx.astype(jnp.int32) + qy.astype(jnp.int32)
    place = (((quad * KMAX + mx) * KMAX + my) * 4).astype(f32)
    for r in range(lines):
        param[2 * lines + r : 2 * lines + r + 1, :] = place[:, r * LANE : (r + 1) * LANE]


def spread_rows(s_ref, param, grid_rows, x_even, x_odd, place_v, place_s, sem, ready=()):
    f32 = jnp.float32
    lines = s_ref.shape[0] // LANE
    place = param[2 * lines : 3 * lines, :].astype(jnp.int32)
    for r in range(lines):
        place_v[0:1, r * LANE : (r + 1) * LANE] = place[r : r + 1, :]
    idx_copy = pltpu.make_async_copy(place_v.at[0], place_s, sem)
    idx_copy.start()

    def turned(r, x_ref):
        here = pl.ds(pl.multiple_of(r * LANE, LANE), LANE)
        ph_c = jnp.broadcast_to(param[pl.ds(r, 1), :], (LANE, LANE)).T
        ph_s = jnp.broadcast_to(param[pl.ds(lines + r, 1), :], (LANE, LANE)).T
        for h in range(2):
            re = s_ref[here, pl.ds(h * LANE, LANE)].astype(f32)
            im = s_ref[here, pl.ds((2 + h) * LANE, LANE)].astype(f32)
            x_ref[pl.ds(h, LANE, stride=4), :] = ph_c * re + ph_s * im
            x_ref[pl.ds(2 + h, LANE, stride=4), :] = ph_c * im - ph_s * re

    def scatter(r, x_ref):
        base = r * LANE
        for u in range(LANE):
            to = pl.multiple_of(place_s[base + u], 4)
            grid_rows[pl.ds(to, 4), :] = x_ref[4 * u : 4 * u + 4, :]

    stops = [last for last, _ in ready] + [lines] if ready else [0, lines]
    waits = [wait for _, wait in ready] if ready else [lambda: None]
    for first, stop, wait in zip(stops, stops[1:], waits):
        wait()
        turned(first, x_even)
        if first == 0:
            idx_copy.wait()

        @pl.loop(first // 2, stop // 2)
        def _(i):
            r = 2 * i
            turned(r + 1, x_odd)
            scatter(r, x_even)
            turned(jnp.minimum(r + 2, stop - 1), x_even)
            scatter(r + 1, x_odd)


def own_kernel(s_own, param, grid_rows, basis, zero, s_vmem, sems, *scratch):
    lines = s_vmem.shape[0] // LANE
    starts = (0, lines // 4)
    ready = []
    for n, (first, stop) in enumerate(zip(starts, starts[1:] + (lines,))):
        part = pl.ds(first * LANE, (stop - first) * LANE)
        load = pltpu.make_async_copy(s_own.at[part], s_vmem.at[part], sems.at[n])
        load.start()
        ready.append((first, load.wait))
    zero[...] = jnp.zeros_like(zero)
    spread_rows(s_vmem, param, grid_rows, *scratch, ready=ready)


def basis_rows(grid_rows, g, basis, at):
    bf16 = jnp.bfloat16
    quarter = KMAX * KMAX * 4
    for h in range(2):
        vals = []
        for part in range(2):
            mm, mp, pm, pp = (
                grid_rows[pl.ds(q * quarter + g * 4 * LANE + 2 * part + h, LANE, stride=4), :] for q in range(4)
            )
            a, c = pp + mm, pm + mp
            b, d = (pp - mm, pm - mp) if part else (mm - pp, mp - pm)
            vals.append((a + c, c - a, b + d, b - d))
        re, im = vals
        at_re, at_im = pl.ds(2 * h * LANE, LANE), pl.ds((2 * h + 1) * LANE, LANE)
        for n in range(4):
            to = pl.ds(pl.multiple_of((4 * at + n) * LANE, LANE), LANE)
            one, two = (re[n], im[n]) if n < 2 else (im[n], re[n])
            basis[to, at_re], basis[to, at_im] = one.astype(bf16), two.astype(bf16)


def other_kernel(held, room, s_rem, param, grid_rows, basis, zero, *scratch):
    zero[...] = jnp.zeros_like(zero)
    spread_rows(s_rem, param, grid_rows, *scratch)

    @pl.loop(0, KMAX * KMAX // LANE)
    def _(g):
        basis_rows(grid_rows, g, basis, g)


def prepare(source, j, coef, tab, sub=32):
    f32, bf16 = jnp.float32, jnp.bfloat16
    half = lax.axis_index("beam")
    step = coef.shape[0]

    def tables(i):
        pos = source[j + i, 32:48, :].astype(f32).astype(jnp.int32)
        pos = 32 * pos[0:4] + pos[4:8]
        pos = jnp.where(half == 0, pos[0:2], pos[2:4])
        px, py = pos[0:1], pos[1:2]
        my = lax.broadcasted_iota(jnp.int32, (KMAX, LANE), 0)
        mx = lax.broadcasted_iota(jnp.int32, (8, LANE), 0)
        cy, sy = half_turns((2 * my + 1) * py)
        cx, sx = half_turns(jnp.where(mx < 4, 2 * mx + 1, 8) * px)
        reps = LANE // KMAX
        spread = lambda t: jnp.concatenate([jnp.broadcast_to(t[m : m + 1], (KMAX, LANE)) for m in range(reps)], 0)
        made = (
            jnp.concatenate([cy] * reps, 0), jnp.concatenate([sy] * reps, 0), spread(cx), spread(sx),
            jnp.broadcast_to(cx[4:5], (LANE, LANE)), jnp.broadcast_to(sx[4:5], (LANE, LANE)),
        )
        for n, t in enumerate(made):
            tab[n, i * LANE : (i + 1) * LANE, :] = t.T

    for i in range(step // LANE):
        tables(i)
    for row in range(0, step, sub):
        cy, sy, cx, sx, c4, s4 = (tab[n, row : row + sub, :] for n in range(6))
        for g in range(KMAX // 4):
            prods = (cx * cy, sx * sy, sx * cy, cx * sy)
            for n, v in enumerate(prods):
                coef[row : row + sub, (4 * g + n) * LANE : (4 * g + n + 1) * LANE] = v.astype(bf16)
            cx, sx = cx * c4 - sx * s4, sx * c4 + cx * s4


def near_kernel(basis, near, psi_near, coef_even, coef_odd, tab_even, tab_odd):
    step = coef_even.shape[0]
    turns = [(coef_even, tab_even), (coef_odd, tab_odd)]
    prepare(near, 0, *turns[0])
    steps = near.shape[0] * LANE // step
    for m in range(steps):
        psi = jnp.dot(turns[m % 2][0][...], basis[...], preferred_element_type=jnp.float32)
        if m + 1 < steps:
            prepare(near, (m + 1) * step // LANE, *turns[(m + 1) % 2])
        psi_near[m * step : (m + 1) * step, :] = psi


def far_kernel(masks, basis, psi_near, near, far, cols, overlap, out, coef_even, coef_odd, tab_even, tab_odd, pots):
    f32, bf16 = jnp.float32, jnp.bfloat16
    column = lax.axis_index("probe")
    step = coef_even.shape[0]
    blocks = near.shape[0]
    mul = lambda a, b: jnp.dot(a, b, preferred_element_type=f32)
    forms = []

    def make_forms():
        for n, source in enumerate((near, far)):
            for j in range(blocks):
                owner = column ^ masks[n * blocks + j]
                pats = source[j, 0:32, :].astype(f32)
                for t in range(4):
                    pots[pl.ds(pl.multiple_of(owner * 8, 8), 8), t * LANE : (t + 1) * LANE] = pats[8 * t : 8 * t + 8]
        mine = (cols[...] == column).astype(f32)
        left = (pots[...].T * mine).astype(bf16)
        right = pots[...].astype(bf16)
        g_re, g_im = overlap[0], overlap[1]
        for h in range(2):
            lr, li = left[h * LANE : (h + 1) * LANE], left[(2 + h) * LANE : (3 + h) * LANE]
            rr, ri = right[:, h * LANE : (h + 1) * LANE], right[:, (2 + h) * LANE : (3 + h) * LANE]
            r_re, r_im = mul(lr, rr) + mul(li, ri), mul(li, rr) - mul(lr, ri)
            h_re, h_im = g_re * r_re - g_im * r_im, g_re * r_im + g_im * r_re
            forms.append(
                jnp.concatenate([jnp.concatenate([h_re, h_im], 1), jnp.concatenate([-h_im, h_re], 1)], 0).astype(bf16)
            )

    def half_energy(wave, h):
        v = wave * mul(wave.astype(bf16), forms[h])
        return v[:, :LANE] + v[:, LANE:]

    def finish(first, e):
        for i in range(step // LANE):
            out[pl.ds(column ^ masks[first + i], 1), :] = jnp.sum(e[i * LANE : (i + 1) * LANE].T, axis=0, keepdims=True)

    turns = [(coef_even, tab_even), (coef_odd, tab_odd)]
    prepare(far, 0, *turns[0])
    cols_of = [slice(2 * h * LANE, (2 * h + 2) * LANE) for h in range(2)]
    units = [(m, h) for m in range(far.shape[0] * LANE // step) for h in range(2)]
    waiting, e = None, 0.0
    for m, h in units + [(None, None)]:
        if m is not None:
            wave = mul(turns[m % 2][0][...], basis[:, cols_of[h]])
            if h == 0 and (m + 1, 0) in units:
                prepare(far, (m + 1) * step // LANE, *turns[(m + 1) % 2])
            if (m, h) == (0, 0):
                make_forms()
            if (m, h) == (0, 1):
                for first in range(0, psi_near.shape[0], step):
                    rows = slice(first, first + step)
                    finish(first // LANE, sum(half_energy(psi_near[rows, cols_of[k]], k) for k in range(2)))
        if waiting is not None:
            old_m, old_h, old = waiting
            part = half_energy(old, old_h)
            e = part if old_h == 0 else e + part
            if old_h == 1:
                finish(blocks + old_m * step // LANE, e)
        waiting = (m, h, wave)


def shards(smatrix, aperture, aberration, beam_k, probe_pos, patches, patch_col):
    f32, bf16 = jnp.float32, jnp.bfloat16
    blocks = lax.axis_size("probe")
    rows, width = smatrix.shape[0], smatrix.shape[2]
    lines, grid = rows // LANE, 4 * KMAX * KMAX
    swap = lambda v: lax.ppermute(v, "beam", [(0, 1), (1, 0)])
    sds = jax.ShapeDtypeStruct
    vmem, hbm = pl.BlockSpec(memory_space=pltpu.VMEM), pl.BlockSpec(memory_space=pltpu.HBM)
    params = pltpu.CompilerParams(vmem_limit_bytes=24 * 1024 * 1024)
    cost = lambda n: pl.CostEstimate(flops=n, bytes_accessed=4 * 2**20, transcendentals=0)

    message = sds((1, 48, LANE), bf16)
    s_own = smatrix.reshape(rows, width)
    raw = (aperture.reshape(lines, LANE), aberration.reshape(lines, LANE), beam_k, probe_pos, patches)
    small, param = pl.pallas_call(
        pack_kernel,
        out_shape=(message, sds((3 * lines, LANE), f32)),
        in_specs=[hbm] * len(raw),
        out_specs=(vmem,) * 2,
        scratch_shapes=[pltpu.VMEM(v.shape, v.dtype) for v in raw] + [pltpu.SemaphoreType.DMA((len(raw),))],
        compiler_params=params,
        cost_estimate=cost(10**9),
    )(*(pltpu.with_memory_space_constraint(v, pltpu.HBM) for v in raw))
    param_rem = swap(param)
    s_rem = swap(s_own)

    turning = [
        pltpu.VMEM((4 * LANE, LANE), f32),
        pltpu.VMEM((4 * LANE, LANE), f32),
        pltpu.VMEM((1, rows), jnp.int32),
        pltpu.SMEM((rows,), jnp.int32),
        pltpu.SemaphoreType.DMA,
    ]
    held_shape = sds((4 * grid, LANE), f32)
    basis_shape = sds((grid, width), bf16)
    held, room, zero_own = pl.pallas_call(
        own_kernel,
        out_shape=(held_shape, basis_shape, message),
        in_specs=[hbm, vmem],
        out_specs=(vmem,) * 3,
        scratch_shapes=[pltpu.VMEM((rows, width), bf16), pltpu.SemaphoreType.DMA((2,))] + turning,
        compiler_params=params,
        cost_estimate=cost(3 * 10**9),
    )(pltpu.with_memory_space_constraint(s_own, pltpu.HBM), param)
    _, basis, zero_other = pl.pallas_call(
        other_kernel,
        out_shape=(held_shape, basis_shape, message),
        in_specs=[vmem] * 4,
        out_specs=(vmem,) * 3,
        scratch_shapes=turning,
        input_output_aliases={0: 0, 1: 1},
        compiler_params=params,
        cost_estimate=cost(4 * 10**9),
    )(held, room, s_rem, param_rem)

    steps = [1 << n for n in range(blocks.bit_length() - 1)]
    steps = steps[-2:] + steps[:-2][::-1]
    beside, masks = [zero_own, zero_other], [0]
    for reach in steps:
        far = lax.ppermute(
            small, ("probe", "beam"), [(2 * i + b, 2 * (i ^ reach) + 1 - b) for i in range(blocks) for b in range(2)]
        )
        masks = masks + [m ^ reach for m in masks]
        near = small
        if reach != steps[-1]:
            small = jnp.concatenate([near, far + beside.pop(0) if beside else far], 0)

    probes = blocks // 2 * LANE
    working = [
        pltpu.VMEM((2 * LANE, grid), bf16),
        pltpu.VMEM((2 * LANE, grid), bf16),
        pltpu.VMEM((6, 2 * LANE, LANE), f32),
        pltpu.VMEM((6, 2 * LANE, LANE), f32),
    ]
    psi_near = pl.pallas_call(
        near_kernel,
        out_shape=sds((probes, width), f32),
        in_specs=[vmem] * 2,
        out_specs=vmem,
        scratch_shapes=working,
        compiler_params=params,
        cost_estimate=cost(4 * 10**9),
    )(basis, near)
    energy = pl.pallas_call(
        functools.partial(far_kernel, tuple(masks)),
        out_shape=jax.ShapeDtypeStruct((blocks, LANE), f32),
        in_specs=[vmem] * 6,
        out_specs=vmem,
        scratch_shapes=working + [pltpu.VMEM((patch_col.shape[0], width), f32)],
        compiler_params=params,
        cost_estimate=cost(4 * 10**9),
    )(basis, psi_near, near, far, patch_col.reshape(1, -1), jnp.asarray(mode_overlap()))
    return lax.all_to_all(energy, "probe", 0, 0, tiled=True)


def solution(mesh):
    placed = (
        P(("grp", "beam"), "probe", None),
        P("beam"),
        P("beam"),
        P(None, "beam"),
        P(None, "probe"),
        P(("grp", "probe"), None),
        P("grp"),
    )
    return jax.shard_map(
        shards, mesh=mesh, in_specs=placed, out_specs=P("grp", ("probe", "beam")), check_vma=False
    )
```

```python
import functools
import math

import jax
import jax.numpy as jnp
import numpy as np
from jax import lax
from jax.experimental import pallas as pl
from jax.experimental.pallas import tpu as pltpu
from jax.sharding import PartitionSpec as P

PSIDE = 16
GRID = 1024
KMAX = 32
LANE = 128


def mode_overlap():
    pix = np.arange(LANE)
    row, col = pix // PSIDE, pix % PSIDE
    dist = col[:, None] - col[None, :]
    freq = np.arange(PSIDE // 2) - PSIDE // 4
    angle = (2.0 * math.pi / PSIDE) * ((freq[:, None, None] * dist[None]) % PSIDE)
    same = (row[:, None] == row[None, :]).astype(np.float64) * PSIDE / float(PSIDE**2 * (PSIDE**2 // 2))
    return np.stack([np.cos(angle).sum(0) * same, -np.sin(angle).sum(0) * same]).astype(np.float32)


def half_turns(count):
    folded = jnp.bitwise_and(count + GRID, 2 * GRID - 1) - GRID
    u = folded.astype(jnp.float32) * (1.0 / GRID)
    u2 = u * u
    terms = 9
    c = [(-1.0) ** k * math.pi ** (2 * k) / math.factorial(2 * k) for k in range(terms)]
    s = [(-1.0) ** k * math.pi ** (2 * k + 1) / math.factorial(2 * k + 1) for k in range(terms)]
    cos_v, sin_v = jnp.full_like(u, c[-1]), jnp.full_like(u, s[-1])
    for k in range(terms - 2, -1, -1):
        cos_v = cos_v * u2 + c[k]
        sin_v = sin_v * u2 + s[k]
    return cos_v, sin_v * u


def pack_kernel(amp, abr, k_hbm, pos_hbm, patches, small, param, amp_v, abr_v, k_v, pos_v, pat_v, sems):
    f32, bf16 = jnp.float32, jnp.bfloat16
    pairs = [(amp, amp_v), (abr, abr_v), (k_hbm, k_v), (pos_hbm, pos_v), (patches, pat_v)]
    copies = [pltpu.make_async_copy(src, dst, sems.at[n]) for n, (src, dst) in enumerate(pairs)]
    for c in copies:
        c.start()
    for c in copies:
        c.wait()
    pats = pat_v[...].astype(f32)
    pos = jnp.concatenate([pos_v[:, :LANE], pos_v[:, LANE:]], 0)
    tiles = [pats[:, t * LANE : (t + 1) * LANE] for t in range(pats.shape[1] // LANE)]
    split = [(pos // 32).astype(f32), (pos % 32).astype(f32)]
    message = jnp.concatenate(tiles + [jnp.concatenate(split, 0)], 0)
    small[0] = message.astype(bf16)
    lines = amp_v.shape[0]
    param[0:lines, :] = amp_v[...] * jnp.cos(abr_v[...])
    param[lines : 2 * lines, :] = amp_v[...] * jnp.sin(abr_v[...])
    kx, ky = k_v[0:1, :], k_v[1:2, :]
    qx, qy = kx >= 0, ky >= 0
    mx, my = jnp.where(qx, kx, -1 - kx), jnp.where(qy, ky, -1 - ky)
    quad = 2 * qx.astype(jnp.int32) + qy.astype(jnp.int32)
    place = (((quad * KMAX + mx) * KMAX + my) * 4).astype(f32)
    for r in range(lines):
        param[2 * lines + r : 2 * lines + r + 1, :] = place[:, r * LANE : (r + 1) * LANE]


def spread_rows(s_ref, param, grid_rows, x_even, x_odd, place_v, place_s, sem, ready=()):
    f32 = jnp.float32
    lines = s_ref.shape[0] // LANE
    place = param[2 * lines : 3 * lines, :].astype(jnp.int32)
    for r in range(lines):
        place_v[0:1, r * LANE : (r + 1) * LANE] = place[r : r + 1, :]
    idx_copy = pltpu.make_async_copy(place_v.at[0], place_s, sem)
    idx_copy.start()

    def turned(r, x_ref):
        here = pl.ds(pl.multiple_of(r * LANE, LANE), LANE)
        ph_c = jnp.broadcast_to(param[pl.ds(r, 1), :], (LANE, LANE)).T
        ph_s = jnp.broadcast_to(param[pl.ds(lines + r, 1), :], (LANE, LANE)).T
        for h in range(2):
            re = s_ref[here, pl.ds(h * LANE, LANE)].astype(f32)
            im = s_ref[here, pl.ds((2 + h) * LANE, LANE)].astype(f32)
            x_ref[pl.ds(h, LANE, stride=4), :] = ph_c * re + ph_s * im
            x_ref[pl.ds(2 + h, LANE, stride=4), :] = ph_c * im - ph_s * re

    def scatter(r, x_ref):
        base = r * LANE
        for u in range(LANE):
            to = pl.multiple_of(place_s[base + u], 4)
            grid_rows[pl.ds(to, 4), :] = x_ref[4 * u : 4 * u + 4, :]

    stops = [last for last, _ in ready] + [lines] if ready else [0, lines]
    waits = [wait for _, wait in ready] if ready else [lambda: None]
    for first, stop, wait in zip(stops, stops[1:], waits):
        wait()
        turned(first, x_even)
        if first == 0:
            idx_copy.wait()

        @pl.loop(first // 2, stop // 2)
        def _(i):
            r = 2 * i
            turned(r + 1, x_odd)
            scatter(r, x_even)
            turned(jnp.minimum(r + 2, stop - 1), x_even)
            scatter(r + 1, x_odd)


def own_kernel(s_own, param, grid_rows, basis, zero, s_vmem, sems, *scratch):
    lines = s_vmem.shape[0] // LANE
    starts = (0, lines // 4)
    ready = []
    for n, (first, stop) in enumerate(zip(starts, starts[1:] + (lines,))):
        part = pl.ds(first * LANE, (stop - first) * LANE)
        load = pltpu.make_async_copy(s_own.at[part], s_vmem.at[part], sems.at[n])
        load.start()
        ready.append((first, load.wait))
    zero[...] = jnp.zeros_like(zero)
    spread_rows(s_vmem, param, grid_rows, *scratch, ready=ready)


def basis_rows(grid_rows, g, basis, at):
    bf16 = jnp.bfloat16
    quarter = KMAX * KMAX * 4
    for h in range(2):
        vals = []
        for part in range(2):
            mm, mp, pm, pp = (
                grid_rows[pl.ds(q * quarter + g * 4 * LANE + 2 * part + h, LANE, stride=4), :] for q in range(4)
            )
            a, c = pp + mm, pm + mp
            b, d = (pp - mm, pm - mp) if part else (mm - pp, mp - pm)
            vals.append((a + c, c - a, b + d, b - d))
        re, im = vals
        at_re, at_im = pl.ds(2 * h * LANE, LANE), pl.ds((2 * h + 1) * LANE, LANE)
        for n in range(4):
            to = pl.ds(pl.multiple_of((4 * at + n) * LANE, LANE), LANE)
            one, two = (re[n], im[n]) if n < 2 else (im[n], re[n])
            basis[to, at_re], basis[to, at_im] = one.astype(bf16), two.astype(bf16)


def other_kernel(held, room, s_rem, param, grid_rows, basis, zero, *scratch):
    zero[...] = jnp.zeros_like(zero)
    spread_rows(s_rem, param, grid_rows, *scratch)

    @pl.loop(0, KMAX * KMAX // LANE // 2)
    def _(g):
        basis_rows(grid_rows, 2 * g, basis, 2 * g)
        basis_rows(grid_rows, 2 * g + 1, basis, 2 * g + 1)


def prepare(source, j, coef, tab, sub=32):
    f32, bf16 = jnp.float32, jnp.bfloat16
    half = lax.axis_index("beam")
    step = coef.shape[0]

    def tables(i):
        pos = source[j + i].astype(f32)[32:40].astype(jnp.int32)
        pos = 32 * pos[0:4] + pos[4:8]
        pos = jnp.where(half == 0, pos[0:2], pos[2:4])
        px, py = pos[0:1], pos[1:2]
        my = lax.broadcasted_iota(jnp.int32, (KMAX, LANE), 0)
        mx = lax.broadcasted_iota(jnp.int32, (8, LANE), 0)
        cy, sy = half_turns((2 * my + 1) * py)
        cx, sx = half_turns(jnp.where(mx < 4, 2 * mx + 1, 8) * px)
        reps = LANE // KMAX
        spread = lambda t: jnp.concatenate([jnp.broadcast_to(t[m : m + 1], (KMAX, LANE)) for m in range(reps)], 0)
        made = (
            jnp.concatenate([cy] * reps, 0), jnp.concatenate([sy] * reps, 0), spread(cx), spread(sx),
            jnp.broadcast_to(cx[4:5], (LANE, LANE)), jnp.broadcast_to(sx[4:5], (LANE, LANE)),
        )
        for n, t in enumerate(made):
            tab[n, i * LANE : (i + 1) * LANE, :] = t.T

    for i in range(step // LANE):
        tables(i)
    for row in range(0, step, sub):
        cy, sy, cx, sx, c4, s4 = (tab[n, row : row + sub, :] for n in range(6))
        for g in range(KMAX // 4):
            prods = (cx * cy, sx * sy, sx * cy, cx * sy)
            for n, v in enumerate(prods):
                coef[row : row + sub, (4 * g + n) * LANE : (4 * g + n + 1) * LANE] = v.astype(bf16)
            cx, sx = cx * c4 - sx * s4, sx * c4 + cx * s4


def near_kernel(basis, near, psi_near, coef_even, coef_odd, tab_even, tab_odd):
    step = coef_even.shape[0]
    turns = [(coef_even, tab_even), (coef_odd, tab_odd)]
    prepare(near, 0, *turns[0])
    steps = near.shape[0] * LANE // step
    for m in range(steps):
        psi = jnp.dot(turns[m % 2][0][...], basis[...], preferred_element_type=jnp.float32)
        if m + 1 < steps:
            prepare(near, (m + 1) * step // LANE, *turns[(m + 1) % 2])
        psi_near[m * step : (m + 1) * step, :] = psi


def far_kernel(masks, basis, psi_near, near, far, cols, overlap, out, coef_even, coef_odd, tab_even, tab_odd, pots):
    f32, bf16 = jnp.float32, jnp.bfloat16
    column = lax.axis_index("probe")
    step = coef_even.shape[0]
    blocks = near.shape[0]
    mul = lambda a, b: jnp.dot(a, b, preferred_element_type=f32)
    forms = []

    def make_forms():
        for n, source in enumerate((near, far)):
            for j in range(blocks):
                owner = column ^ masks[n * blocks + j]
                pats = source[j].astype(f32)
                for t in range(4):
                    pots[pl.ds(pl.multiple_of(owner * 8, 8), 8), t * LANE : (t + 1) * LANE] = pats[8 * t : 8 * t + 8]
        mine = (cols[...] == column).astype(f32)
        left = (pots[...].T * mine).astype(bf16)
        right = pots[...].astype(bf16)
        g_re, g_im = overlap[0], overlap[1]
        for h in range(2):
            lr, li = left[h * LANE : (h + 1) * LANE], left[(2 + h) * LANE : (3 + h) * LANE]
            rr, ri = right[:, h * LANE : (h + 1) * LANE], right[:, (2 + h) * LANE : (3 + h) * LANE]
            r_re, r_im = mul(lr, rr) + mul(li, ri), mul(li, rr) - mul(lr, ri)
            h_re, h_im = g_re * r_re - g_im * r_im, g_re * r_im + g_im * r_re
            forms.append(
                jnp.concatenate([jnp.concatenate([h_re, h_im], 1), jnp.concatenate([-h_im, h_re], 1)], 0).astype(bf16)
            )

    def half_energy(wave, h):
        v = wave * mul(wave.astype(bf16), forms[h])
        return v[:, :LANE] + v[:, LANE:]

    def finish(first, e):
        for i in range(step // LANE):
            out[pl.ds(column ^ masks[first + i], 1), :] = jnp.sum(e[i * LANE : (i + 1) * LANE].T, axis=0, keepdims=True)

    turns = [(coef_even, tab_even), (coef_odd, tab_odd)]
    prepare(far, 0, *turns[0])
    cols_of = [slice(2 * h * LANE, (2 * h + 2) * LANE) for h in range(2)]
    units = [(m, h) for m in range(far.shape[0] * LANE // step) for h in range(2)]
    waiting, e = None, 0.0
    for m, h in units + [(None, None)]:
        if m is not None:
            wave = mul(turns[m % 2][0][...], basis[:, cols_of[h]])
            if h == 0 and (m + 1, 0) in units:
                prepare(far, (m + 1) * step // LANE, *turns[(m + 1) % 2])
            if (m, h) == (0, 0):
                make_forms()
            if (m, h) == (0, 1):
                for first in range(0, psi_near.shape[0], step):
                    rows = slice(first, first + step)
                    finish(first // LANE, sum(half_energy(psi_near[rows, cols_of[k]], k) for k in range(2)))
        if waiting is not None:
            old_m, old_h, old = waiting
            part = half_energy(old, old_h)
            e = part if old_h == 0 else e + part
            if old_h == 1:
                finish(blocks + old_m * step // LANE, e)
        waiting = (m, h, wave)


def shards(smatrix, aperture, aberration, beam_k, probe_pos, patches, patch_col):
    f32, bf16 = jnp.float32, jnp.bfloat16
    blocks = lax.axis_size("probe")
    rows, width = smatrix.shape[0], smatrix.shape[2]
    lines, grid = rows // LANE, 4 * KMAX * KMAX
    swap = lambda v: lax.ppermute(v, "beam", [(0, 1), (1, 0)])
    sds = jax.ShapeDtypeStruct
    vmem, hbm = pl.BlockSpec(memory_space=pltpu.VMEM), pl.BlockSpec(memory_space=pltpu.HBM)
    params = pltpu.CompilerParams(vmem_limit_bytes=24 * 1024 * 1024)
    cost = lambda n: pl.CostEstimate(flops=n, bytes_accessed=4 * 2**20, transcendentals=0)

    message = sds((1, 40, LANE), bf16)
    s_own = smatrix.reshape(rows, width)
    raw = (aperture.reshape(lines, LANE), aberration.reshape(lines, LANE), beam_k, probe_pos, patches)
    small, param = pl.pallas_call(
        pack_kernel,
        out_shape=(message, sds((3 * lines, LANE), f32)),
        in_specs=[hbm] * len(raw),
        out_specs=(vmem,) * 2,
        scratch_shapes=[pltpu.VMEM(v.shape, v.dtype) for v in raw] + [pltpu.SemaphoreType.DMA((len(raw),))],
        compiler_params=params,
        cost_estimate=cost(10**9),
    )(*(pltpu.with_memory_space_constraint(v, pltpu.HBM) for v in raw))
    param_rem = swap(param)
    s_rem = swap(s_own)

    turning = [
        pltpu.VMEM((4 * LANE, LANE), f32),
        pltpu.VMEM((4 * LANE, LANE), f32),
        pltpu.VMEM((1, rows), jnp.int32),
        pltpu.SMEM((rows,), jnp.int32),
        pltpu.SemaphoreType.DMA,
    ]
    held_shape = sds((4 * grid, LANE), f32)
    basis_shape = sds((grid, width), bf16)
    held, room, zero_own = pl.pallas_call(
        own_kernel,
        out_shape=(held_shape, basis_shape, message),
        in_specs=[hbm, vmem],
        out_specs=(vmem,) * 3,
        scratch_shapes=[pltpu.VMEM((rows, width), bf16), pltpu.SemaphoreType.DMA((2,))] + turning,
        compiler_params=params,
        cost_estimate=cost(3 * 10**9),
    )(pltpu.with_memory_space_constraint(s_own, pltpu.HBM), param)
    _, basis, zero_other = pl.pallas_call(
        other_kernel,
        out_shape=(held_shape, basis_shape, message),
        in_specs=[vmem] * 4,
        out_specs=(vmem,) * 3,
        scratch_shapes=turning,
        input_output_aliases={0: 0, 1: 1},
        compiler_params=params,
        cost_estimate=cost(4 * 10**9),
    )(held, room, s_rem, param_rem)

    steps = [1 << n for n in range(blocks.bit_length() - 1)]
    steps = steps[-2:] + steps[:-2][::-1]
    beside, masks = [zero_own, zero_other], [0]
    for reach in steps:
        far = lax.ppermute(
            small, ("probe", "beam"), [(2 * i + b, 2 * (i ^ reach) + 1 - b) for i in range(blocks) for b in range(2)]
        )
        masks = masks + [m ^ reach for m in masks]
        near = small
        if reach != steps[-1]:
            small = jnp.concatenate([near, far + beside.pop(0) if beside else far], 0)

    probes = blocks // 2 * LANE
    working = [
        pltpu.VMEM((2 * LANE, grid), bf16),
        pltpu.VMEM((2 * LANE, grid), bf16),
        pltpu.VMEM((6, 2 * LANE, LANE), f32),
        pltpu.VMEM((6, 2 * LANE, LANE), f32),
    ]
    psi_near = pl.pallas_call(
        near_kernel,
        out_shape=sds((probes, width), f32),
        in_specs=[vmem] * 2,
        out_specs=vmem,
        scratch_shapes=working,
        compiler_params=params,
        cost_estimate=cost(4 * 10**9),
    )(basis, near)
    energy = pl.pallas_call(
        functools.partial(far_kernel, tuple(masks)),
        out_shape=jax.ShapeDtypeStruct((blocks, LANE), f32),
        in_specs=[vmem] * 6,
        out_specs=vmem,
        scratch_shapes=working + [pltpu.VMEM((patch_col.shape[0], width), f32)],
        compiler_params=params,
        cost_estimate=cost(4 * 10**9),
    )(basis, psi_near, near, far, patch_col.reshape(1, -1), jnp.asarray(mode_overlap()))
    return lax.all_to_all(energy, "probe", 0, 0, tiled=True)


def solution(mesh):
    placed = (
        P(("grp", "beam"), "probe", None),
        P("beam"),
        P("beam"),
        P(None, "beam"),
        P(None, "probe"),
        P(("grp", "probe"), None),
        P("grp"),
    )
    return jax.shard_map(
        shards, mesh=mesh, in_specs=placed, out_specs=P("grp", ("probe", "beam")), check_vma=False
    )
```

```python
import functools
import math

import jax
import jax.numpy as jnp
import numpy as np
from jax import lax
from jax.experimental import pallas as pl
from jax.experimental.pallas import tpu as pltpu
from jax.sharding import PartitionSpec as P

PSIDE = 16
GRID = 1024
KMAX = 32
LANE = 128


def mode_overlap():
    pix = np.arange(LANE)
    row, col = pix // PSIDE, pix % PSIDE
    dist = col[:, None] - col[None, :]
    freq = np.arange(PSIDE // 2) - PSIDE // 4
    angle = (2.0 * math.pi / PSIDE) * ((freq[:, None, None] * dist[None]) % PSIDE)
    same = (row[:, None] == row[None, :]).astype(np.float64) * PSIDE / float(PSIDE**2 * (PSIDE**2 // 2))
    return np.stack([np.cos(angle).sum(0) * same, -np.sin(angle).sum(0) * same]).astype(np.float32)


def half_turns(count):
    folded = jnp.bitwise_and(count + GRID, 2 * GRID - 1) - GRID
    u = folded.astype(jnp.float32) * (1.0 / GRID)
    u2 = u * u
    terms = 9
    c = [(-1.0) ** k * math.pi ** (2 * k) / math.factorial(2 * k) for k in range(terms)]
    s = [(-1.0) ** k * math.pi ** (2 * k + 1) / math.factorial(2 * k + 1) for k in range(terms)]
    cos_v, sin_v = jnp.full_like(u, c[-1]), jnp.full_like(u, s[-1])
    for k in range(terms - 2, -1, -1):
        cos_v = cos_v * u2 + c[k]
        sin_v = sin_v * u2 + s[k]
    return cos_v, sin_v * u


def pack_kernel(amp, abr, k_hbm, pos_hbm, patches, small, param, amp_v, abr_v, k_v, pos_v, pat_v, sems):
    f32, bf16 = jnp.float32, jnp.bfloat16
    pairs = [(amp, amp_v), (abr, abr_v), (k_hbm, k_v), (pos_hbm, pos_v), (patches, pat_v)]
    copies = [pltpu.make_async_copy(src, dst, sems.at[n]) for n, (src, dst) in enumerate(pairs)]
    for c in copies:
        c.start()
    for c in copies:
        c.wait()
    pats = pat_v[...].astype(f32)
    pos = jnp.concatenate([pos_v[:, :LANE], pos_v[:, LANE:]], 0)
    tiles = [pats[:, t * LANE : (t + 1) * LANE] for t in range(pats.shape[1] // LANE)]
    split = [(pos // 32).astype(f32), (pos % 32).astype(f32)]
    message = jnp.concatenate(tiles + [jnp.concatenate(split, 0)], 0)
    small[0] = message.astype(bf16)
    lines = amp_v.shape[0]
    param[0:lines, :] = amp_v[...] * jnp.cos(abr_v[...])
    param[lines : 2 * lines, :] = amp_v[...] * jnp.sin(abr_v[...])
    kx, ky = k_v[0:1, :], k_v[1:2, :]
    qx, qy = kx >= 0, ky >= 0
    mx, my = jnp.where(qx, kx, -1 - kx), jnp.where(qy, ky, -1 - ky)
    quad = 2 * qx.astype(jnp.int32) + qy.astype(jnp.int32)
    place = (((quad * KMAX + mx) * KMAX + my) * 4).astype(f32)
    for r in range(lines):
        param[2 * lines + r : 2 * lines + r + 1, :] = place[:, r * LANE : (r + 1) * LANE]


def spread_rows(s_ref, param, grid_rows, x_even, x_odd, place_v, place_s, sem, ready=()):
    f32 = jnp.float32
    lines = s_ref.shape[0] // LANE
    place = param[2 * lines : 3 * lines, :].astype(jnp.int32)
    for r in range(lines):
        place_v[0:1, r * LANE : (r + 1) * LANE] = place[r : r + 1, :]
    idx_copy = pltpu.make_async_copy(place_v.at[0], place_s, sem)
    idx_copy.start()

    def turned(r, x_ref):
        here = pl.ds(pl.multiple_of(r * LANE, LANE), LANE)
        ph_c = jnp.broadcast_to(param[pl.ds(r, 1), :], (LANE, LANE)).T
        ph_s = jnp.broadcast_to(param[pl.ds(lines + r, 1), :], (LANE, LANE)).T
        for h in range(2):
            re = s_ref[here, pl.ds(h * LANE, LANE)].astype(f32)
            im = s_ref[here, pl.ds((2 + h) * LANE, LANE)].astype(f32)
            x_ref[pl.ds(h, LANE, stride=4), :] = ph_c * re + ph_s * im
            x_ref[pl.ds(2 + h, LANE, stride=4), :] = ph_c * im - ph_s * re

    def scatter(r, x_ref):
        base = r * LANE
        for u in range(LANE):
            to = pl.multiple_of(place_s[base + u], 4)
            grid_rows[pl.ds(to, 4), :] = x_ref[4 * u : 4 * u + 4, :]

    stops = [last for last, _ in ready] + [lines] if ready else [0, lines]
    waits = [wait for _, wait in ready] if ready else [lambda: None]
    for first, stop, wait in zip(stops, stops[1:], waits):
        wait()
        turned(first, x_even)
        if first == 0:
            idx_copy.wait()

        @pl.loop(first // 2, stop // 2)
        def _(i):
            r = 2 * i
            turned(r + 1, x_odd)
            scatter(r, x_even)
            turned(jnp.minimum(r + 2, stop - 1), x_even)
            scatter(r + 1, x_odd)


def own_kernel(s_own, param, grid_rows, basis, zero, s_vmem, sems, *scratch):
    lines = s_vmem.shape[0] // LANE
    starts = (0, lines // 4)
    ready = []
    for n, (first, stop) in enumerate(zip(starts, starts[1:] + (lines,))):
        part = pl.ds(first * LANE, (stop - first) * LANE)
        load = pltpu.make_async_copy(s_own.at[part], s_vmem.at[part], sems.at[n])
        load.start()
        ready.append((first, load.wait))
    zero[...] = jnp.zeros_like(zero)
    spread_rows(s_vmem, param, grid_rows, *scratch, ready=ready)


def basis_rows(grid_rows, g, basis, at):
    bf16 = jnp.bfloat16
    quarter = KMAX * KMAX * 4
    for h in range(2):
        vals = []
        for part in range(2):
            mm, mp, pm, pp = (
                grid_rows[pl.ds(q * quarter + g * 4 * LANE + 2 * part + h, LANE, stride=4), :] for q in range(4)
            )
            a, c = pp + mm, pm + mp
            b, d = (pp - mm, pm - mp) if part else (mm - pp, mp - pm)
            vals.append((a + c, c - a, b + d, b - d))
        re, im = vals
        at_re, at_im = pl.ds(2 * h * LANE, LANE), pl.ds((2 * h + 1) * LANE, LANE)
        for n in range(4):
            to = pl.ds(pl.multiple_of((4 * at + n) * LANE, LANE), LANE)
            one, two = (re[n], im[n]) if n < 2 else (im[n], re[n])
            basis[to, at_re], basis[to, at_im] = one.astype(bf16), two.astype(bf16)


def other_kernel(held, room, s_rem, param, grid_rows, basis, zero, *scratch):
    zero[...] = jnp.zeros_like(zero)
    spread_rows(s_rem, param, grid_rows, *scratch)

    @pl.loop(0, KMAX * KMAX // LANE // 2)
    def _(g):
        basis_rows(grid_rows, 2 * g, basis, 2 * g)
        basis_rows(grid_rows, 2 * g + 1, basis, 2 * g + 1)


def prepare(source, j, coef, tab, sub=32):
    f32, bf16 = jnp.float32, jnp.bfloat16
    half = lax.axis_index("beam")
    step = coef.shape[0]

    def tables(i):
        pos = source[j + i].astype(f32)[32:40].astype(jnp.int32)
        pos = 32 * pos[0:4] + pos[4:8]
        pos = jnp.where(half == 0, pos[0:2], pos[2:4])
        px, py = pos[0:1], pos[1:2]
        my = lax.broadcasted_iota(jnp.int32, (KMAX, LANE), 0)
        mx = lax.broadcasted_iota(jnp.int32, (8, LANE), 0)
        cy, sy = half_turns((2 * my + 1) * py)
        cx, sx = half_turns(jnp.where(mx < 4, 2 * mx + 1, 8) * px)
        reps = LANE // KMAX
        spread = lambda t: jnp.concatenate([jnp.broadcast_to(t[m : m + 1], (KMAX, LANE)) for m in range(reps)], 0)
        made = (
            jnp.concatenate([cy] * reps, 0), jnp.concatenate([sy] * reps, 0), spread(cx), spread(sx),
            jnp.broadcast_to(cx[4:5], (LANE, LANE)), jnp.broadcast_to(sx[4:5], (LANE, LANE)),
        )
        for n, t in enumerate(made):
            tab[n, i * LANE : (i + 1) * LANE, :] = t.T

    for i in range(step // LANE):
        tables(i)
    for row in range(0, step, sub):
        cy, sy, cx, sx, c4, s4 = (tab[n, row : row + sub, :] for n in range(6))
        for g in range(KMAX // 4):
            prods = (cx * cy, sx * sy, sx * cy, cx * sy)
            for n, v in enumerate(prods):
                coef[row : row + sub, (4 * g + n) * LANE : (4 * g + n + 1) * LANE] = v.astype(bf16)
            cx, sx = cx * c4 - sx * s4, sx * c4 + cx * s4


def near_kernel(basis, near, psi_near, coef_even, coef_odd, tab_even, tab_odd):
    step = coef_even.shape[0]
    turns = [(coef_even, tab_even), (coef_odd, tab_odd)]
    prepare(near, 0, *turns[0])
    steps = near.shape[0] * LANE // step
    for m in range(steps):
        psi = jnp.dot(turns[m % 2][0][...], basis[...], preferred_element_type=jnp.float32)
        if m + 1 < steps:
            prepare(near, (m + 1) * step // LANE, *turns[(m + 1) % 2])
        psi_near[m * step : (m + 1) * step, :] = psi


def far_kernel(masks, basis, psi_near, near, far, cols, overlap, out, coef_even, coef_odd, tab_even, tab_odd, pots):
    f32, bf16 = jnp.float32, jnp.bfloat16
    column = lax.axis_index("probe")
    step = coef_even.shape[0]
    blocks = near.shape[0]
    mul = lambda a, b: jnp.dot(a, b, preferred_element_type=f32)
    forms = []

    def make_forms():
        for n, source in enumerate((near, far)):
            for j in range(blocks):
                owner = column ^ masks[n * blocks + j]
                pats = source[j].astype(f32)
                for t in range(4):
                    pots[pl.ds(pl.multiple_of(owner * 8, 8), 8), t * LANE : (t + 1) * LANE] = pats[8 * t : 8 * t + 8]
        mine = (cols[...] == column).astype(f32)
        left = (pots[...].T * mine).astype(bf16)
        right = pots[...].astype(bf16)
        g_re, g_im = overlap[0], overlap[1]
        for h in range(2):
            lr, li = left[h * LANE : (h + 1) * LANE], left[(2 + h) * LANE : (3 + h) * LANE]
            rr, ri = right[:, h * LANE : (h + 1) * LANE], right[:, (2 + h) * LANE : (3 + h) * LANE]
            r_re, r_im = mul(lr, rr) + mul(li, ri), mul(li, rr) - mul(lr, ri)
            h_re, h_im = g_re * r_re - g_im * r_im, g_re * r_im + g_im * r_re
            forms.append(
                jnp.concatenate([jnp.concatenate([h_re, h_im], 1), jnp.concatenate([-h_im, h_re], 1)], 0).astype(bf16)
            )

    def half_energy(wave, h):
        v = wave * mul(wave.astype(bf16), forms[h])
        return v[:, :LANE] + v[:, LANE:]

    def finish(first, e):
        for i in range(step // LANE):
            out[pl.ds(column ^ masks[first + i], 1), :] = jnp.sum(e[i * LANE : (i + 1) * LANE].T, axis=0, keepdims=True)

    turns = [(coef_even, tab_even), (coef_odd, tab_odd)]
    prepare(far, 0, *turns[0])
    cols_of = [slice(2 * h * LANE, (2 * h + 2) * LANE) for h in range(2)]
    units = [(m, h) for m in range(far.shape[0] * LANE // step) for h in range(2)]
    waiting, e = None, 0.0
    for m, h in units + [(None, None)]:
        if m is not None:
            wave = mul(turns[m % 2][0][...], basis[:, cols_of[h]])
            if h == 0 and (m + 1, 0) in units:
                prepare(far, (m + 1) * step // LANE, *turns[(m + 1) % 2])
            if (m, h) == (0, 0):
                make_forms()
            if (m, h) == (0, 1):
                for first in range(0, psi_near.shape[0], step):
                    rows = slice(first, first + step)
                    finish(first // LANE, sum(half_energy(psi_near[rows, cols_of[k]], k) for k in range(2)))
        if waiting is not None:
            old_m, old_h, old = waiting
            part = half_energy(old, old_h)
            e = part if old_h == 0 else e + part
            if old_h == 1:
                finish(blocks + old_m * step // LANE, e)
        waiting = (m, h, wave)


def shards(smatrix, aperture, aberration, beam_k, probe_pos, patches, patch_col):
    f32, bf16 = jnp.float32, jnp.bfloat16
    blocks = lax.axis_size("probe")
    rows, width = smatrix.shape[0], smatrix.shape[2]
    lines, grid = rows // LANE, 4 * KMAX * KMAX
    swap = lambda v: lax.ppermute(v, "beam", [(0, 1), (1, 0)])
    sds = jax.ShapeDtypeStruct
    vmem, hbm = pl.BlockSpec(memory_space=pltpu.VMEM), pl.BlockSpec(memory_space=pltpu.HBM)
    params = pltpu.CompilerParams(vmem_limit_bytes=24 * 1024 * 1024)
    cost = lambda n: pl.CostEstimate(flops=n, bytes_accessed=4 * 2**20, transcendentals=0)

    message = sds((1, 40, LANE), bf16)
    s_own = smatrix.reshape(rows, width)
    raw = (aperture.reshape(lines, LANE), aberration.reshape(lines, LANE), beam_k, probe_pos, patches)
    small, param = pl.pallas_call(
        pack_kernel,
        out_shape=(message, sds((3 * lines, LANE), f32)),
        in_specs=[hbm] * len(raw),
        out_specs=(vmem,) * 2,
        scratch_shapes=[pltpu.VMEM(v.shape, v.dtype) for v in raw] + [pltpu.SemaphoreType.DMA((len(raw),))],
        compiler_params=params,
        cost_estimate=cost(10**9),
    )(*(pltpu.with_memory_space_constraint(v, pltpu.HBM) for v in raw))
    param_rem = swap(param)
    later, _ = lax.optimization_barrier((s_own, small))
    s_rem = swap(later)

    turning = [
        pltpu.VMEM((4 * LANE, LANE), f32),
        pltpu.VMEM((4 * LANE, LANE), f32),
        pltpu.VMEM((1, rows), jnp.int32),
        pltpu.SMEM((rows,), jnp.int32),
        pltpu.SemaphoreType.DMA,
    ]
    held_shape = sds((4 * grid, LANE), f32)
    basis_shape = sds((grid, width), bf16)
    held, room, zero_own = pl.pallas_call(
        own_kernel,
        out_shape=(held_shape, basis_shape, message),
        in_specs=[hbm, vmem],
        out_specs=(vmem,) * 3,
        scratch_shapes=[pltpu.VMEM((rows, width), bf16), pltpu.SemaphoreType.DMA((2,))] + turning,
        compiler_params=params,
        cost_estimate=cost(3 * 10**9),
    )(pltpu.with_memory_space_constraint(s_own, pltpu.HBM), param)
    _, basis, zero_other = pl.pallas_call(
        other_kernel,
        out_shape=(held_shape, basis_shape, message),
        in_specs=[vmem] * 4,
        out_specs=(vmem,) * 3,
        scratch_shapes=turning,
        input_output_aliases={0: 0, 1: 1},
        compiler_params=params,
        cost_estimate=cost(4 * 10**9),
    )(held, room, s_rem, param_rem)

    steps = [1 << n for n in range(blocks.bit_length() - 1)]
    steps = steps[-2:] + steps[:-2][::-1]
    beside, masks = [zero_own, zero_other], [0]
    for reach in steps:
        far = lax.ppermute(
            small, ("probe", "beam"), [(2 * i + b, 2 * (i ^ reach) + 1 - b) for i in range(blocks) for b in range(2)]
        )
        masks = masks + [m ^ reach for m in masks]
        near = small
        if reach != steps[-1]:
            small = jnp.concatenate([near, far + beside.pop(0) if beside else far], 0)

    probes = blocks // 2 * LANE
    working = [
        pltpu.VMEM((2 * LANE, grid), bf16),
        pltpu.VMEM((2 * LANE, grid), bf16),
        pltpu.VMEM((6, 2 * LANE, LANE), f32),
        pltpu.VMEM((6, 2 * LANE, LANE), f32),
    ]
    psi_near = pl.pallas_call(
        near_kernel,
        out_shape=sds((probes, width), f32),
        in_specs=[vmem] * 2,
        out_specs=vmem,
        scratch_shapes=working,
        compiler_params=params,
        cost_estimate=cost(4 * 10**9),
    )(basis, near)
    energy = pl.pallas_call(
        functools.partial(far_kernel, tuple(masks)),
        out_shape=jax.ShapeDtypeStruct((blocks, LANE), f32),
        in_specs=[vmem] * 6,
        out_specs=vmem,
        scratch_shapes=working + [pltpu.VMEM((patch_col.shape[0], width), f32)],
        compiler_params=params,
        cost_estimate=cost(4 * 10**9),
    )(basis, psi_near, near, far, patch_col.reshape(1, -1), jnp.asarray(mode_overlap()))
    return lax.all_to_all(energy, "probe", 0, 0, tiled=True)


def solution(mesh):
    placed = (
        P(("grp", "beam"), "probe", None),
        P("beam"),
        P("beam"),
        P(None, "beam"),
        P(None, "probe"),
        P(("grp", "probe"), None),
        P("grp"),
    )
    return jax.shard_map(
        shards, mesh=mesh, in_specs=placed, out_specs=P("grp", ("probe", "beam")), check_vma=False
    )
```

```python
import functools
import math

import jax
import jax.numpy as jnp
import numpy as np
from jax import lax
from jax.experimental import pallas as pl
from jax.experimental.pallas import tpu as pltpu
from jax.sharding import PartitionSpec as P

PSIDE = 16
GRID = 1024
KMAX = 32
LANE = 128


def mode_overlap():
    pix = np.arange(LANE)
    row, col = pix // PSIDE, pix % PSIDE
    dist = col[:, None] - col[None, :]
    freq = np.arange(PSIDE // 2) - PSIDE // 4
    angle = (2.0 * math.pi / PSIDE) * ((freq[:, None, None] * dist[None]) % PSIDE)
    same = (row[:, None] == row[None, :]).astype(np.float64) * PSIDE / float(PSIDE**2 * (PSIDE**2 // 2))
    return np.stack([np.cos(angle).sum(0) * same, -np.sin(angle).sum(0) * same]).astype(np.float32)


def half_turns(count):
    folded = jnp.bitwise_and(count + GRID, 2 * GRID - 1) - GRID
    u = folded.astype(jnp.float32) * (1.0 / GRID)
    u2 = u * u
    terms = 9
    c = [(-1.0) ** k * math.pi ** (2 * k) / math.factorial(2 * k) for k in range(terms)]
    s = [(-1.0) ** k * math.pi ** (2 * k + 1) / math.factorial(2 * k + 1) for k in range(terms)]
    cos_v, sin_v = jnp.full_like(u, c[-1]), jnp.full_like(u, s[-1])
    for k in range(terms - 2, -1, -1):
        cos_v = cos_v * u2 + c[k]
        sin_v = sin_v * u2 + s[k]
    return cos_v, sin_v * u


def pack_kernel(amp, abr, k_hbm, pos_hbm, patches, small, param, amp_v, abr_v, k_v, pos_v, pat_v, sems):
    f32, bf16 = jnp.float32, jnp.bfloat16
    pairs = [(amp, amp_v), (abr, abr_v), (k_hbm, k_v), (pos_hbm, pos_v), (patches, pat_v)]
    copies = [pltpu.make_async_copy(src, dst, sems.at[n]) for n, (src, dst) in enumerate(pairs)]
    for c in copies:
        c.start()
    for c in copies:
        c.wait()
    pats = pat_v[...].astype(f32)
    pos = jnp.concatenate([pos_v[:, :LANE], pos_v[:, LANE:]], 0)
    tiles = [pats[:, t * LANE : (t + 1) * LANE] for t in range(pats.shape[1] // LANE)]
    split = [(pos // 32).astype(f32), (pos % 32).astype(f32), jnp.zeros((8, LANE), f32)]
    message = jnp.concatenate(tiles + [jnp.concatenate(split, 0)], 0)
    small[0] = message.astype(bf16)
    lines = amp_v.shape[0]
    param[0:lines, :] = amp_v[...] * jnp.cos(abr_v[...])
    param[lines : 2 * lines, :] = amp_v[...] * jnp.sin(abr_v[...])
    kx, ky = k_v[0:1, :], k_v[1:2, :]
    qx, qy = kx >= 0, ky >= 0
    mx, my = jnp.where(qx, kx, -1 - kx), jnp.where(qy, ky, -1 - ky)
    quad = 2 * qx.astype(jnp.int32) + qy.astype(jnp.int32)
    place = (((quad * KMAX + mx) * KMAX + my) * 4).astype(f32)
    for r in range(lines):
        param[2 * lines + r : 2 * lines + r + 1, :] = place[:, r * LANE : (r + 1) * LANE]


def spread_rows(s_ref, param, grid_rows, x_even, x_odd, place_v, place_s, sem, ready=()):
    f32 = jnp.float32
    lines = s_ref.shape[0] // LANE
    place = param[2 * lines : 3 * lines, :].astype(jnp.int32)
    for r in range(lines):
        place_v[0:1, r * LANE : (r + 1) * LANE] = place[r : r + 1, :]
    idx_copy = pltpu.make_async_copy(place_v.at[0], place_s, sem)
    idx_copy.start()

    def turned(r, x_ref):
        here = pl.ds(pl.multiple_of(r * LANE, LANE), LANE)
        ph_c = jnp.broadcast_to(param[pl.ds(r, 1), :], (LANE, LANE)).T
        ph_s = jnp.broadcast_to(param[pl.ds(lines + r, 1), :], (LANE, LANE)).T
        for h in range(2):
            re = s_ref[here, pl.ds(h * LANE, LANE)].astype(f32)
            im = s_ref[here, pl.ds((2 + h) * LANE, LANE)].astype(f32)
            x_ref[pl.ds(h, LANE, stride=4), :] = ph_c * re + ph_s * im
            x_ref[pl.ds(2 + h, LANE, stride=4), :] = ph_c * im - ph_s * re

    def scatter(r, x_ref):
        base = r * LANE
        for u in range(LANE):
            to = pl.multiple_of(place_s[base + u], 4)
            grid_rows[pl.ds(to, 4), :] = x_ref[4 * u : 4 * u + 4, :]

    stops = [last for last, _ in ready] + [lines] if ready else [0, lines]
    waits = [wait for _, wait in ready] if ready else [lambda: None]
    for first, stop, wait in zip(stops, stops[1:], waits):
        wait()
        turned(first, x_even)
        if first == 0:
            idx_copy.wait()

        @pl.loop(first // 2, stop // 2)
        def _(i):
            r = 2 * i
            turned(r + 1, x_odd)
            scatter(r, x_even)
            turned(jnp.minimum(r + 2, stop - 1), x_even)
            scatter(r + 1, x_odd)


def own_kernel(s_own, param, grid_rows, basis, zero, s_vmem, sems, *scratch):
    lines = s_vmem.shape[0] // LANE
    starts = (0, lines // 4)
    ready = []
    for n, (first, stop) in enumerate(zip(starts, starts[1:] + (lines,))):
        part = pl.ds(first * LANE, (stop - first) * LANE)
        load = pltpu.make_async_copy(s_own.at[part], s_vmem.at[part], sems.at[n])
        load.start()
        ready.append((first, load.wait))
    zero[...] = jnp.zeros_like(zero)
    spread_rows(s_vmem, param, grid_rows, *scratch, ready=ready)


def basis_rows(grid_rows, g, basis, at):
    bf16 = jnp.bfloat16
    quarter = KMAX * KMAX * 4
    for h in range(2):
        vals = []
        for part in range(2):
            mm, mp, pm, pp = (
                grid_rows[pl.ds(q * quarter + g * 4 * LANE + 2 * part + h, LANE, stride=4), :] for q in range(4)
            )
            a, c = pp + mm, pm + mp
            b, d = (pp - mm, pm - mp) if part else (mm - pp, mp - pm)
            vals.append((a + c, c - a, b + d, b - d))
        re, im = vals
        at_re, at_im = pl.ds(2 * h * LANE, LANE), pl.ds((2 * h + 1) * LANE, LANE)
        for n in range(4):
            to = pl.ds(pl.multiple_of((4 * at + n) * LANE, LANE), LANE)
            one, two = (re[n], im[n]) if n < 2 else (im[n], re[n])
            basis[to, at_re], basis[to, at_im] = one.astype(bf16), two.astype(bf16)


def other_kernel(held, room, s_rem, param, grid_rows, basis, zero, *scratch):
    zero[...] = jnp.zeros_like(zero)
    spread_rows(s_rem, param, grid_rows, *scratch)

    @pl.loop(0, KMAX * KMAX // LANE // 2)
    def _(g):
        basis_rows(grid_rows, 2 * g, basis, 2 * g)
        basis_rows(grid_rows, 2 * g + 1, basis, 2 * g + 1)


def prepare(source, j, coef, tab, sub=32):
    f32, bf16 = jnp.float32, jnp.bfloat16
    half = lax.axis_index("beam")
    step = coef.shape[0]

    def tables(i):
        pos = source[j + i, 32:48, :].astype(f32).astype(jnp.int32)
        pos = 32 * pos[0:4] + pos[4:8]
        pos = jnp.where(half == 0, pos[0:2], pos[2:4])
        px, py = pos[0:1], pos[1:2]
        my = lax.broadcasted_iota(jnp.int32, (KMAX, LANE), 0)
        mx = lax.broadcasted_iota(jnp.int32, (8, LANE), 0)
        cy, sy = half_turns((2 * my + 1) * py)
        cx, sx = half_turns(jnp.where(mx < 4, 2 * mx + 1, 8) * px)
        reps = LANE // KMAX
        spread = lambda t: jnp.concatenate([jnp.broadcast_to(t[m : m + 1], (KMAX, LANE)) for m in range(reps)], 0)
        made = (
            jnp.concatenate([cy] * reps, 0), jnp.concatenate([sy] * reps, 0), spread(cx), spread(sx),
            jnp.broadcast_to(cx[4:5], (LANE, LANE)), jnp.broadcast_to(sx[4:5], (LANE, LANE)),
        )
        for n, t in enumerate(made):
            tab[n, i * LANE : (i + 1) * LANE, :] = t.T

    for i in range(step // LANE):
        tables(i)
    for row in range(0, step, sub):
        cy, sy, cx, sx, c4, s4 = (tab[n, row : row + sub, :] for n in range(6))
        for g in range(KMAX // 4):
            prods = (cx * cy, sx * sy, sx * cy, cx * sy)
            for n, v in enumerate(prods):
                coef[row : row + sub, (4 * g + n) * LANE : (4 * g + n + 1) * LANE] = v.astype(bf16)
            cx, sx = cx * c4 - sx * s4, sx * c4 + cx * s4


def near_kernel(basis, near, psi_near, coef_even, coef_odd, tab_even, tab_odd):
    step = coef_even.shape[0]
    turns = [(coef_even, tab_even), (coef_odd, tab_odd)]
    prepare(near, 0, *turns[0])
    steps = near.shape[0] * LANE // step
    for m in range(steps):
        psi = jnp.dot(turns[m % 2][0][...], basis[...], preferred_element_type=jnp.float32)
        if m + 1 < steps:
            prepare(near, (m + 1) * step // LANE, *turns[(m + 1) % 2])
        psi_near[m * step : (m + 1) * step, :] = psi


def far_kernel(masks, basis, psi_near, near, far, cols, overlap, out, coef_even, coef_odd, tab_even, tab_odd, pots):
    f32, bf16 = jnp.float32, jnp.bfloat16
    column = lax.axis_index("probe")
    step = coef_even.shape[0]
    blocks = near.shape[0]
    mul = lambda a, b: jnp.dot(a, b, preferred_element_type=f32)
    forms = []

    def make_forms():
        for n, source in enumerate((near, far)):
            for j in range(blocks):
                owner = column ^ masks[n * blocks + j]
                pats = source[j, 0:32, :].astype(f32)
                for t in range(4):
                    pots[pl.ds(pl.multiple_of(owner * 8, 8), 8), t * LANE : (t + 1) * LANE] = pats[8 * t : 8 * t + 8]
        mine = (cols[...] == column).astype(f32)
        left = (pots[...].T * mine).astype(bf16)
        right = pots[...].astype(bf16)
        g_re, g_im = overlap[0], overlap[1]
        for h in range(2):
            lr, li = left[h * LANE : (h + 1) * LANE], left[(2 + h) * LANE : (3 + h) * LANE]
            rr, ri = right[:, h * LANE : (h + 1) * LANE], right[:, (2 + h) * LANE : (3 + h) * LANE]
            r_re, r_im = mul(lr, rr) + mul(li, ri), mul(li, rr) - mul(lr, ri)
            h_re, h_im = g_re * r_re - g_im * r_im, g_re * r_im + g_im * r_re
            forms.append(
                jnp.concatenate([jnp.concatenate([h_re, h_im], 1), jnp.concatenate([-h_im, h_re], 1)], 0).astype(bf16)
            )

    def half_energy(wave, h):
        v = wave * mul(wave.astype(bf16), forms[h])
        return v[:, :LANE] + v[:, LANE:]

    def finish(first, e):
        for i in range(step // LANE):
            out[pl.ds(column ^ masks[first + i], 1), :] = jnp.sum(e[i * LANE : (i + 1) * LANE].T, axis=0, keepdims=True)

    turns = [(coef_even, tab_even), (coef_odd, tab_odd)]
    prepare(far, 0, *turns[0])
    cols_of = [slice(2 * h * LANE, (2 * h + 2) * LANE) for h in range(2)]
    units = [(m, h) for m in range(far.shape[0] * LANE // step) for h in range(2)]
    waiting, e = None, 0.0
    for m, h in units + [(None, None)]:
        if m is not None:
            wave = mul(turns[m % 2][0][...], basis[:, cols_of[h]])
            if h == 0 and (m + 1, 0) in units:
                prepare(far, (m + 1) * step // LANE, *turns[(m + 1) % 2])
            if (m, h) == (0, 0):
                make_forms()
            if (m, h) == (0, 1):
                for first in range(0, psi_near.shape[0], step):
                    rows = slice(first, first + step)
                    finish(first // LANE, sum(half_energy(psi_near[rows, cols_of[k]], k) for k in range(2)))
        if waiting is not None:
            old_m, old_h, old = waiting
            part = half_energy(old, old_h)
            e = part if old_h == 0 else e + part
            if old_h == 1:
                finish(blocks + old_m * step // LANE, e)
        waiting = (m, h, wave)


def shards(smatrix, aperture, aberration, beam_k, probe_pos, patches, patch_col):
    f32, bf16 = jnp.float32, jnp.bfloat16
    blocks = lax.axis_size("probe")
    rows, width = smatrix.shape[0], smatrix.shape[2]
    lines, grid = rows // LANE, 4 * KMAX * KMAX
    swap = lambda v: lax.ppermute(v, "beam", [(0, 1), (1, 0)])
    sds = jax.ShapeDtypeStruct
    vmem, hbm = pl.BlockSpec(memory_space=pltpu.VMEM), pl.BlockSpec(memory_space=pltpu.HBM)
    params = pltpu.CompilerParams(vmem_limit_bytes=24 * 1024 * 1024)
    cost = lambda n: pl.CostEstimate(flops=n, bytes_accessed=4 * 2**20, transcendentals=0)

    message = sds((1, 48, LANE), bf16)
    s_own = smatrix.reshape(rows, width)
    raw = (aperture.reshape(lines, LANE), aberration.reshape(lines, LANE), beam_k, probe_pos, patches)
    small, param = pl.pallas_call(
        pack_kernel,
        out_shape=(message, sds((3 * lines, LANE), f32)),
        in_specs=[hbm] * len(raw),
        out_specs=(vmem,) * 2,
        scratch_shapes=[pltpu.VMEM(v.shape, v.dtype) for v in raw] + [pltpu.SemaphoreType.DMA((len(raw),))],
        compiler_params=params,
        cost_estimate=cost(10**9),
    )(*(pltpu.with_memory_space_constraint(v, pltpu.HBM) for v in raw))
    param_rem = swap(param)
    later, _ = lax.optimization_barrier((s_own, small))
    s_rem = swap(later)

    turning = [
        pltpu.VMEM((4 * LANE, LANE), f32),
        pltpu.VMEM((4 * LANE, LANE), f32),
        pltpu.VMEM((1, rows), jnp.int32),
        pltpu.SMEM((rows,), jnp.int32),
        pltpu.SemaphoreType.DMA,
    ]
    held_shape = sds((4 * grid, LANE), f32)
    basis_shape = sds((grid, width), bf16)
    held, room, zero_own = pl.pallas_call(
        own_kernel,
        out_shape=(held_shape, basis_shape, message),
        in_specs=[hbm, vmem],
        out_specs=(vmem,) * 3,
        scratch_shapes=[pltpu.VMEM((rows, width), bf16), pltpu.SemaphoreType.DMA((2,))] + turning,
        compiler_params=params,
        cost_estimate=cost(3 * 10**9),
    )(pltpu.with_memory_space_constraint(s_own, pltpu.HBM), param)
    _, basis, zero_other = pl.pallas_call(
        other_kernel,
        out_shape=(held_shape, basis_shape, message),
        in_specs=[vmem] * 4,
        out_specs=(vmem,) * 3,
        scratch_shapes=turning,
        input_output_aliases={0: 0, 1: 1},
        compiler_params=params,
        cost_estimate=cost(4 * 10**9),
    )(held, room, s_rem, param_rem)

    steps = [1 << n for n in range(blocks.bit_length() - 1)]
    steps = steps[-2:] + steps[:-2][::-1]
    beside, masks = [zero_own, zero_other], [0]
    for reach in steps:
        far = lax.ppermute(
            small, ("probe", "beam"), [(2 * i + b, 2 * (i ^ reach) + 1 - b) for i in range(blocks) for b in range(2)]
        )
        masks = masks + [m ^ reach for m in masks]
        near = small
        if reach != steps[-1]:
            small = jnp.concatenate([near, far + beside.pop(0) if beside else far], 0)

    probes = blocks // 2 * LANE
    working = [
        pltpu.VMEM((2 * LANE, grid), bf16),
        pltpu.VMEM((2 * LANE, grid), bf16),
        pltpu.VMEM((6, 2 * LANE, LANE), f32),
        pltpu.VMEM((6, 2 * LANE, LANE), f32),
    ]
    psi_near = pl.pallas_call(
        near_kernel,
        out_shape=sds((probes, width), f32),
        in_specs=[vmem] * 2,
        out_specs=vmem,
        scratch_shapes=working,
        compiler_params=params,
        cost_estimate=cost(4 * 10**9),
    )(basis, near)
    energy = pl.pallas_call(
        functools.partial(far_kernel, tuple(masks)),
        out_shape=jax.ShapeDtypeStruct((blocks, LANE), f32),
        in_specs=[vmem] * 6,
        out_specs=vmem,
        scratch_shapes=working + [pltpu.VMEM((patch_col.shape[0], width), f32)],
        compiler_params=params,
        cost_estimate=cost(4 * 10**9),
    )(basis, psi_near, near, far, patch_col.reshape(1, -1), jnp.asarray(mode_overlap()))
    return lax.all_to_all(energy, "probe", 0, 0, tiled=True)


def solution(mesh):
    placed = (
        P(("grp", "beam"), "probe", None),
        P("beam"),
        P("beam"),
        P(None, "beam"),
        P(None, "probe"),
        P(("grp", "probe"), None),
        P("grp"),
    )
    return jax.shard_map(
        shards, mesh=mesh, in_specs=placed, out_specs=P("grp", ("probe", "beam")), check_vma=False
    )
```
